256 devices in a mesh: queue: 32 (over z_lo, x, core), head: 8 (over y, z_hi).
Axes of the slice: x: 4, y: 4, z: 8 (z_hi: 2, z_lo: 4; z = z_hi * 4 + z_lo), core: 2. Of those that a mesh axis runs over, the one named last changes fastest.
Arguments:
- latents: bfloat16 [128, 192, 3072], P('queue', 'head'), may hold values from -1.5 to 1.5
- queries: bfloat16 [128, 192, 3072], P('queue', 'head'), may hold values from -100 to 100
- key_proj: bfloat16 [128, 192, 3072], P('queue', 'head'), may hold values from -6.75 to 6.75
- values: bfloat16 [128, 192, 3072], P('queue', 'head'), may hold values from -48 to 48
- slot_steps: int32 [128], P('queue'), may hold values from 0 to 127
- noise_frame: bfloat16 [192, 3072], P('head'), may hold values from -6 to 6
Outputs:
- queue_next: bfloat16 [128, 192, 3072], P('queue', 'head')
- denoised: bfloat16 [128, 192, 3072], P('queue', 'head')
- finished: bfloat16 [192, 3072], P('head', 'queue')
The draws below stay inside these ranges and needn't reach their ends.
All inputs are finite; a program needn't handle non-finite values.
Results may differ from the reference program's by a relative error of at most 0.007.
Values may be sent and summed in bfloat16 or wider, within the bound.
A program may use at most 128 MiB of HBM per device.

```python
import math
import jax
import jax.numpy as jnp
from jax import lax

HEADS = 24
HEAD_DIM = 128
D = 3072
FRAMES = 4
TOK_FRAME = 192
QUEUE_FRAMES = 128
STEPS = 128
N_QUEUE = 32


def shared_basis(key):
    return jnp.clip(jax.random.normal(key, (QUEUE_FRAMES, TOK_FRAME, D), jnp.float32), -5.0, 5.0)


def draw_key_proj(key, part):
    basis = shared_basis(key)
    return basis.astype(jnp.bfloat16)


def draw_queries(key, part):
    key = jax.random.fold_in(key, 3)
    fresh = jnp.clip(2.0 * jax.random.normal(key, (QUEUE_FRAMES, TOK_FRAME, D), jnp.float32), -10.0, 10.0)
    return fresh.astype(jnp.bfloat16)


def place_ends(values, stream_key, low, largest):
    extent = values.shape
    spot = [jax.random.randint(jax.random.fold_in(stream_key, axis), (), 0, extent[axis]) for axis in range(len(extent))]
    values = values.at[tuple(spot)].set(low)
    longest = extent.index(max(extent))
    spot[longest] = (spot[longest] + 1) % extent[longest]
    return values.at[tuple(spot)].set(largest)


def block_levels(own_key, shape, shards, least, top_value):
    factor_of = 1.0
    for dim, shards_of in shards:
        heights = jax.random.uniform(jax.random.fold_in(jax.random.fold_in(own_key, 6), dim), (shards_of,), jnp.float32, least / len(shards), top_value / len(shards))
        factor_of = factor_of * jnp.repeat(jnp.exp(heights), shape[dim] // shards_of).reshape((-1,) + (1,) * (len(shape) - 1 - dim))
    return factor_of


def noise(stream_key, shape, spread, limit, cuts=(), kind=jnp.bfloat16):
    entries = jax.random.normal(stream_key, shape, jnp.float32) * spread
    if len(cuts) > 0:
        entries = block_levels(stream_key, shape, cuts, -0.22, 0.18) * entries
    return jnp.clip(entries, min=-limit, max=limit).astype(kind)


def setup_inputs(seed: int = 0) -> dict:
    key_of = jax.random.split(jax.random.key(seed), 7)
    return {
        "latents": noise(key_of[0], (QUEUE_FRAMES, TOK_FRAME, D), 0.25, 1.5, ((0, 32), (1, 8))),
        "queries": draw_queries(jax.random.fold_in(key_of[6], 71), 0),
        "key_proj": draw_key_proj(jax.random.fold_in(key_of[6], 71), 0),
        "values": noise(key_of[3], (QUEUE_FRAMES, TOK_FRAME, D), 8.0, 48.0, ((0, 32), (1, 8))),
        "slot_steps": place_ends(jax.random.randint(key_of[4], (QUEUE_FRAMES,), 0, STEPS), jax.random.fold_in(key_of[4], 1), 0, STEPS - 1).astype(jnp.int32),
        "noise_frame": noise(key_of[5], (TOK_FRAME, D), 1.0, 6.0, ((0, 8),)),
    }


shift_factor = 3.0

def noise_level(step_index, total):
    fraction = 1.0 - step_index.astype(jnp.float32) / total
    return shift_factor * fraction / (1.0 + (shift_factor - 1.0) * fraction)

def reference(latents, queries, key_proj, values, slot_steps, noise_frame):
    scale = 1.0 / math.sqrt(HEAD_DIM)
    border = jnp.zeros((FRAMES, TOK_FRAME, D), key_proj.dtype)
    keys_padded = jnp.concatenate([border, key_proj, border], 0)
    values_padded = jnp.concatenate([border, values, border], 0)
    query_count = FRAMES * TOK_FRAME
    key_count = 3 * FRAMES * TOK_FRAME

    def one_window(window):
        start = (window * FRAMES).astype(jnp.int32)
        query_rows = lax.dynamic_slice_in_dim(queries, start, FRAMES, 0).reshape(query_count, HEADS, HEAD_DIM)
        key_rows = lax.dynamic_slice_in_dim(keys_padded, start, 3 * FRAMES, 0).reshape(key_count, HEADS, HEAD_DIM)
        value_rows = lax.dynamic_slice_in_dim(values_padded, start, 3 * FRAMES, 0).reshape(key_count, HEADS, HEAD_DIM)
        block_id = jnp.arange(key_count).astype(jnp.int32) // query_count
        allowed = ((block_id != 0) | (window > 0)) & ((block_id != 2) | (window < N_QUEUE - 1))

        def one_head(head):
            query_head = lax.dynamic_index_in_dim(query_rows, head, 1, keepdims=False)
            key_head = lax.dynamic_index_in_dim(key_rows, head, 1, keepdims=False)
            value_head = lax.dynamic_index_in_dim(value_rows, head, 1, keepdims=False)
            scores = jnp.dot(query_head, key_head.T, preferred_element_type=jnp.float32) * scale
            scores = jnp.where(allowed[None, :], scores, -jnp.inf)
            top = lax.optimization_barrier(jnp.max(scores, axis=1, keepdims=True))
            weights = jnp.where(allowed[None, :], jnp.exp(scores - top), 0.0)
            total = lax.optimization_barrier(jnp.sum(weights, axis=1, keepdims=True))
            mixed = jnp.dot(weights.astype(jnp.bfloat16), value_head, preferred_element_type=jnp.float32)
            return mixed / total
        heads_out = lax.map(one_head, jnp.arange(HEADS).astype(jnp.int32))
        return heads_out.transpose(1, 0, 2).reshape(FRAMES, TOK_FRAME, D).astype(jnp.bfloat16)
    velocity = lax.map(one_window, jnp.arange(N_QUEUE).astype(jnp.int32)).reshape(QUEUE_FRAMES, TOK_FRAME, D)
    velocity_wide = lax.optimization_barrier(velocity).astype(jnp.float32)
    level = noise_level(slot_steps, STEPS)[:, None, None]
    level_next = noise_level(slot_steps + 1, STEPS)[:, None, None]
    latent_wide = latents.astype(jnp.float32)
    updated = (latent_wide + (level_next - level) * velocity_wide).astype(jnp.bfloat16)
    denoised = (latent_wide - level * velocity_wide).astype(jnp.bfloat16)
    queue_next = jnp.concatenate([noise_frame[None], updated[:-1]], 0)
    finished = updated[-1]
    return (queue_next, denoised, finished)
```

```python
import functools
import math

import jax
import jax.numpy as jnp
from jax import lax
from jax.experimental import pallas as pl
from jax.experimental.pallas import tpu as pltpu
from jax.sharding import PartitionSpec as P

MESH = pl.DeviceIdType.MESH
HEADS = 24
HEAD_DIM = 128
D = HEADS * HEAD_DIM
FRAMES = 4
TOKENS = 24
ROWS = FRAMES * TOKENS
SHARES = 8
CLASSES = 3
WINDOW = ROWS * SHARES
CONTEXT = 3 * WINDOW
N_QUEUE = 32
STEPS = 128
HALF = N_QUEUE // 2
CHUNK = 256
PAD = 32
COLUMNS = D // N_QUEUE
SCALE = math.log2(math.e) / math.sqrt(HEAD_DIM)
shift_factor = 3.0


def noise_level(step_index):
    fraction = 1.0 - step_index / float(STEPS)
    return shift_factor * fraction / (1.0 + (shift_factor - 1.0) * fraction)


def kernel(
    q_hbm, k_hbm, v_hbm, lat_hbm, noise_ref, steps_ref,
    next_ref, den_ref, fin_ref,
    qbuf, kbuf, vbuf, obuf, vel, lat, leave, arrive, fin_stage, fin_land,
    send_q, send_k, send_v, recv_q, recv_k, recv_v,
    send_n, recv_kl, recv_kr, recv_vl, recv_vr,
    send_o, recv_o, send_l, recv_l, send_f, recv_f, lat_sem,
):
    q = lax.axis_index("queue")
    h = lax.axis_index("head")
    y, z_hi = h // 2, h % 2
    z_lo = q // 8
    far = (q + HALF) % N_QUEUE

    def flip(window):
        return (window // 16) % 2

    s_mine = (z_hi + flip(far)) % 2
    site_id = y * 2 + s_mine
    window = far

    def site_of(win, ident):
        return ((win + HALF) % N_QUEUE, (ident // 2) * 2 + (ident + flip(win)) % 2)

    has_left = window > 0
    has_right = window < N_QUEUE - 1
    left_site = site_of((window + N_QUEUE - 1) % N_QUEUE, site_id)
    right_site = site_of((window + 1) % N_QUEUE, site_id)

    lat_copy = pltpu.make_async_copy(lat_hbm, lat, lat_sem)
    lat_copy.start()

    barrier = pltpu.get_barrier_semaphore()

    def greet(device):
        pl.semaphore_signal(barrier, inc=1, device_id=device, device_id_type=MESH)

    @pl.loop(0, SHARES)
    def _(i):
        greet((far, i))

    @pl.when(has_left)
    def _():
        greet(left_site)

    @pl.when(has_right)
    def _():
        greet(right_site)

    @pl.when(q > 0)
    def _():
        greet((q - 1, h))

    @pl.when(q < N_QUEUE - 1)
    def _():
        greet((q + 1, h))
        greet((N_QUEUE - 1, h))

    @pl.when(q == N_QUEUE - 1)
    def _():
        @pl.loop(0, N_QUEUE - 1)
        def _(i):
            greet((i, h))

    edges = SHARES + has_left.astype(jnp.int32) + has_right.astype(jnp.int32)
    edges = edges + (q > 0).astype(jnp.int32) + 2 * (q < N_QUEUE - 1).astype(jnp.int32)
    edges = edges + (N_QUEUE - 1) * (q == N_QUEUE - 1).astype(jnp.int32)
    pl.semaphore_wait(barrier, edges)

    def scatter(src, dst, send, recv, j, row0):
        @pl.loop(0, SHARES)
        def _(i):
            column = pl.multiple_of((i * CLASSES + j) * HEAD_DIM, HEAD_DIM)
            row = pl.multiple_of(row0 + h * ROWS, 16)
            pltpu.make_async_remote_copy(
                src_ref=src.at[:, pl.ds(column, HEAD_DIM)],
                dst_ref=dst.at[j, pl.ds(row, ROWS), :],
                send_sem=send,
                recv_sem=recv.at[j],
                device_id=site_of(q, i),
                device_id_type=MESH,
            ).start()

    def scatter_class(j):
        scatter(k_hbm, kbuf, send_k, recv_k, j, WINDOW)
        scatter(v_hbm, vbuf, send_v, recv_v, j, WINDOW)
        scatter(q_hbm, qbuf, send_q, recv_q, j, 0)

    def await_recv(ref, sem):
        pltpu.make_async_copy(ref, ref, sem).wait()

    def own(buf, j):
        return buf.at[j, pl.ds(WINDOW, WINDOW), :]

    def pass_on(buf, j, side, recv, device, slot):
        return pltpu.make_async_remote_copy(
            src_ref=own(buf, j),
            dst_ref=buf.at[j, pl.ds(slot * WINDOW, WINDOW), :],
            send_sem=send_n.at[side, j],
            recv_sem=recv.at[j],
            device_id=device,
            device_id_type=MESH,
        )

    def forward(j):
        for n, (buf, recv, recv_left, recv_right) in enumerate(
            ((kbuf, recv_k, recv_kl, recv_kr), (vbuf, recv_v, recv_vl, recv_vr))
        ):
            await_recv(own(buf, j), recv.at[j])

            @pl.when(has_right)
            def _():
                pass_on(buf, j, 2 * n, recv_left, right_site, 0).start()

            @pl.when(has_left)
            def _():
                pass_on(buf, j, 2 * n + 1, recv_right, left_site, 2).start()

    left_flag = has_left.astype(jnp.float32)
    right_flag = has_right.astype(jnp.float32)

    def gather_context(j):
        @pl.when(has_left)
        def _():
            await_recv(kbuf.at[j, pl.ds(0, WINDOW), :], recv_kl.at[j])
            await_recv(vbuf.at[j, pl.ds(0, WINDOW), :], recv_vl.at[j])

        @pl.when(jnp.logical_not(has_left))
        def _():
            kbuf[j, 0:WINDOW, :] = kbuf[j, WINDOW:2 * WINDOW, :]
            vbuf[j, 0:WINDOW, :] = jnp.zeros((WINDOW, HEAD_DIM), jnp.bfloat16)

        @pl.when(has_right)
        def _():
            await_recv(kbuf.at[j, pl.ds(2 * WINDOW, WINDOW), :], recv_kr.at[j])
            await_recv(vbuf.at[j, pl.ds(2 * WINDOW, WINDOW), :], recv_vr.at[j])

        @pl.when(jnp.logical_not(has_right))
        def _():
            kbuf[j, 2 * WINDOW:, :] = kbuf[j, WINDOW:2 * WINDOW, :]
            vbuf[j, 2 * WINDOW:, :] = jnp.zeros((WINDOW, HEAD_DIM), jnp.bfloat16)

    def attend(j):
        await_recv(qbuf.at[j], recv_q.at[j])

        @pl.loop(0, WINDOW // CHUNK)
        def _(c):
            rows = pl.ds(pl.multiple_of(c * CHUNK, CHUNK), CHUNK)
            scores = lax.dot_general(
                qbuf[j, rows, :], kbuf[j], (((1,), (1,)), ((), ())),
                preferred_element_type=jnp.float32,
            )
            top = jnp.max(scores, axis=1, keepdims=True)
            weights = jnp.exp2((scores - top) * SCALE)
            total = (
                left_flag * jnp.sum(weights[:, :WINDOW], axis=1, keepdims=True)
                + jnp.sum(weights[:, WINDOW:2 * WINDOW], axis=1, keepdims=True)
                + right_flag * jnp.sum(weights[:, 2 * WINDOW:], axis=1, keepdims=True)
            )
            mixed = jnp.dot(
                weights.astype(jnp.bfloat16), vbuf[j], preferred_element_type=jnp.float32
            )
            obuf[j, rows, :] = (mixed / total).astype(jnp.bfloat16)

    def give_back(j):
        @pl.loop(0, SHARES)
        def _(i):
            column = pl.multiple_of(site_id * HEAD_DIM, HEAD_DIM)
            row = pl.multiple_of(i * ROWS, 16)
            pltpu.make_async_remote_copy(
                src_ref=obuf.at[j, pl.ds(row, ROWS), :],
                dst_ref=vel.at[j, :, pl.ds(column, HEAD_DIM)],
                send_sem=send_o.at[j],
                recv_sem=recv_o.at[j],
                device_id=(far, i),
                device_id_type=MESH,
            ).start()

    def levels():
        now, change = [], []
        for f in range(FRAMES):
            step = jnp.full((TOKENS, HEAD_DIM), steps_ref[f], jnp.int32)
            level = noise_level(step.astype(jnp.float32))
            level_next = noise_level((step + 1).astype(jnp.float32))
            now.append(level)
            change.append(level_next - level)
        return now, change

    def update(j):
        await_recv(obuf.at[j], recv_o.at[j])
        now, change = levels()
        for i in range(SHARES):
            head = slice((i * CLASSES + j) * HEAD_DIM, (i * CLASSES + j + 1) * HEAD_DIM)
            block = slice(i * HEAD_DIM, (i + 1) * HEAD_DIM)
            speed = vel[j, :, block].astype(jnp.float32)
            latent = lat[:, head].astype(jnp.float32)
            for f in range(FRAMES):
                frame = slice(f * TOKENS, (f + 1) * TOKENS)
                updated = (latent[frame] + change[f] * speed[frame]).astype(jnp.bfloat16)
                den_ref[f, :, head] = (latent[frame] - now[f] * speed[frame]).astype(jnp.bfloat16)
                if f < FRAMES - 1:
                    next_ref[f + 1, :, head] = updated
                else:
                    leave[j, 0:TOKENS, block] = updated

        @pl.when(q < N_QUEUE - 1)
        def _():
            frame_copy(j).start()

    def frame_copy(j):
        return pltpu.make_async_remote_copy(
            src_ref=leave.at[j],
            dst_ref=arrive.at[j],
            send_sem=send_l.at[j],
            recv_sem=recv_l.at[j],
            device_id=((q + 1) % N_QUEUE, h),
            device_id_type=MESH,
        )

    leave[:, TOKENS:, :] = jnp.zeros((CLASSES, PAD - TOKENS, SHARES * HEAD_DIM), jnp.bfloat16)

    scatter_class(0)
    scatter_class(1)
    forward(0)
    scatter_class(2)
    gather_context(0)
    attend(0)
    give_back(0)
    forward(1)
    gather_context(1)
    attend(1)
    give_back(1)
    forward(2)
    lat_copy.wait()
    update(0)
    gather_context(2)
    attend(2)
    give_back(2)
    update(1)
    update(2)

    def fin_copy(i):
        return pltpu.make_async_remote_copy(
            src_ref=fin_stage.at[i],
            dst_ref=fin_land,
            send_sem=send_f,
            recv_sem=recv_f,
            device_id=(i, h),
            device_id_type=MESH,
        )

    @pl.when(q == N_QUEUE - 1)
    def _():
        fin_stage[:, TOKENS:, :] = jnp.zeros((N_QUEUE, PAD - TOKENS, HEAD_DIM), jnp.bfloat16)
        for i in range(SHARES):
            block = slice(i * HEAD_DIM, (i + 1) * HEAD_DIM)
            wide = jnp.concatenate(
                [leave[j, 0:TOKENS, block].astype(jnp.float32) for j in range(CLASSES)], axis=1
            )
            for p in range(4):
                piece = wide[:, p * COLUMNS:(p + 1) * COLUMNS].astype(jnp.bfloat16)
                fin_stage[4 * i + p, 0:TOKENS, 0:COLUMNS] = piece
                fin_stage[4 * i + p, 0:TOKENS, COLUMNS:] = jnp.zeros(
                    (TOKENS, HEAD_DIM - COLUMNS), jnp.bfloat16
                )

        @pl.loop(0, N_QUEUE - 1)
        def _(i):
            fin_copy(i).start()

        fin_ref[...] = fin_stage[N_QUEUE - 1, 0:TOKENS, 0:COLUMNS]

    @pl.when(q == 0)
    def _():
        next_ref[0] = noise_ref[...]

    @pl.when(q > 0)
    def _():
        for j in range(CLASSES):
            frame_copy(j).wait_recv()
            for i in range(SHARES):
                head = slice((i * CLASSES + j) * HEAD_DIM, (i * CLASSES + j + 1) * HEAD_DIM)
                next_ref[0, :, head] = arrive[j, 0:TOKENS, i * HEAD_DIM:(i + 1) * HEAD_DIM]

    @pl.when(q < N_QUEUE - 1)
    def _():
        await_recv(fin_land, recv_f)
        fin_ref[...] = fin_land[0:TOKENS, 0:COLUMNS]

    await_recv(q_hbm, send_q)
    await_recv(k_hbm, send_k)
    await_recv(v_hbm, send_v)
    for j in range(CLASSES):
        await_recv(obuf.at[j], send_o.at[j])

        @pl.when(has_right)
        def _():
            await_recv(own(kbuf, j), send_n.at[0, j])
            await_recv(own(vbuf, j), send_n.at[2, j])

        @pl.when(has_left)
        def _():
            await_recv(own(kbuf, j), send_n.at[1, j])
            await_recv(own(vbuf, j), send_n.at[3, j])

        @pl.when(q < N_QUEUE - 1)
        def _():
            frame_copy(j).wait_send()

    @pl.when(q == N_QUEUE - 1)
    def _():
        await_recv(fin_stage.at[pl.ds(0, N_QUEUE - 1)], send_f)


def shards(latents, queries, key_proj, values, slot_steps, noise_frame):
    def flat(array):
        return array.reshape(ROWS, D)

    anywhere = pl.BlockSpec(memory_space=pl.ANY)
    vmem = pl.BlockSpec(memory_space=pltpu.VMEM)
    bf16 = jnp.bfloat16
    dma = pltpu.SemaphoreType.DMA
    return pl.pallas_call(
        kernel,
        out_shape=(
            jax.ShapeDtypeStruct((FRAMES, TOKENS, D), bf16),
            jax.ShapeDtypeStruct((FRAMES, TOKENS, D), bf16),
            jax.ShapeDtypeStruct((TOKENS, COLUMNS), bf16),
        ),
        in_specs=[anywhere] * 4 + [vmem, pl.BlockSpec(memory_space=pltpu.SMEM)],
        out_specs=(vmem, vmem, vmem),
        scratch_shapes=[
            pltpu.VMEM((CLASSES, WINDOW, HEAD_DIM), bf16),
            pltpu.VMEM((CLASSES, CONTEXT, HEAD_DIM), bf16),
            pltpu.VMEM((CLASSES, CONTEXT, HEAD_DIM), bf16),
            pltpu.VMEM((CLASSES, WINDOW, HEAD_DIM), bf16),
            pltpu.VMEM((CLASSES, ROWS, SHARES * HEAD_DIM), bf16),
            pltpu.VMEM((ROWS, D), bf16),
            pltpu.VMEM((CLASSES, PAD, SHARES * HEAD_DIM), bf16),
            pltpu.VMEM((CLASSES, PAD, SHARES * HEAD_DIM), bf16),
            pltpu.VMEM((N_QUEUE, PAD, HEAD_DIM), bf16),
            pltpu.VMEM((PAD, HEAD_DIM), bf16),
            dma, dma, dma,
            dma((CLASSES,)), dma((CLASSES,)), dma((CLASSES,)),
            dma((4, CLASSES)),
            dma((CLASSES,)), dma((CLASSES,)), dma((CLASSES,)), dma((CLASSES,)),
            dma((CLASSES,)), dma((CLASSES,)),
            dma((CLASSES,)), dma((CLASSES,)),
            dma, dma, dma,
        ],
        compiler_params=pltpu.CompilerParams(
            collective_id=0, has_side_effects=True, vmem_limit_bytes=48 * 1024 * 1024
        ),
    )(flat(queries), flat(key_proj), flat(values), flat(latents), noise_frame, slot_steps)


def solution(mesh):
    spec = P("queue", "head", None)
    return jax.shard_map(
        shards,
        mesh=mesh,
        in_specs=(spec, spec, spec, spec, P("queue"), P("head", None)),
        out_specs=(spec, spec, P("head", "queue")),
        check_vma=False,
    )
```

```python
import functools
import math

import jax
import jax.numpy as jnp
from jax import lax
from jax.experimental import pallas as pl
from jax.experimental.pallas import tpu as pltpu
from jax.sharding import PartitionSpec as P

MESH = pl.DeviceIdType.MESH
HEADS = 24
HEAD_DIM = 128
D = HEADS * HEAD_DIM
FRAMES = 4
TOKENS = 24
ROWS = FRAMES * TOKENS
SHARES = 8
CLASSES = 3
WINDOW = ROWS * SHARES
CONTEXT = 3 * WINDOW
N_QUEUE = 32
STEPS = 128
HALF = N_QUEUE // 2
CHUNK = 192
PIECE = WINDOW // 4
PAD = 32
COLUMNS = D // N_QUEUE
SCALE = math.log2(math.e) / math.sqrt(HEAD_DIM)
shift_factor = 3.0


def noise_level(step_index):
    fraction = 1.0 - step_index / float(STEPS)
    return shift_factor * fraction / (1.0 + (shift_factor - 1.0) * fraction)


def kernel(
    q_hbm, k_hbm, v_hbm, lat_hbm, noise_hbm, steps_hbm,
    next_ref, den_ref, fin_ref,
    qbuf, kbuf, vbuf, obuf, vel, lat, leave, arrive, fin_stage, fin_land, relayed, steps_ref,
    send_q, send_k, send_v, recv_q, recv_k, recv_v,
    send_n, recv_n, send_r, recv_r,
    send_o, recv_o, send_l, recv_l, send_f, recv_f, lat_sem, noise_sem, steps_sem,
):
    q = lax.axis_index("queue")
    h = lax.axis_index("head")
    y, z_hi = h // 2, h % 2
    z_lo = q // 8
    far = (q + HALF) % N_QUEUE

    def flip(window):
        return (window // 16) % 2

    s_mine = (z_hi + flip(far)) % 2
    site_id = y * 2 + s_mine
    window = far

    def site_of(win, ident):
        return ((win + HALF) % N_QUEUE, (ident // 2) * 2 + (ident + flip(win)) % 2)

    group, place = window // 8, window % 8
    has_left = window > 0
    has_right = window < N_QUEUE - 1
    last = jnp.logical_and(place == 7, has_right)
    first = jnp.logical_and(place == 0, has_left)
    plain_right = place < 7
    plain_left = place > 0
    up = jnp.logical_and(jnp.logical_and(place % 2 == 1, place < 7), group < 3)
    down = jnp.logical_and(jnp.logical_and(place % 2 == 0, place > 0), group > 0)
    is_relay = jnp.logical_or(up, down)
    relay_from = site_of(jnp.where(up, 8 * group + 7, 8 * group), site_id)
    relay_to = site_of(jnp.where(up, 8 * group + 8, (8 * group + N_QUEUE - 1) % N_QUEUE) % N_QUEUE, site_id)

    def relay_up(grp, p):
        return site_of((8 * grp + 2 * p + 1) % N_QUEUE, site_id)

    def relay_down(grp, p):
        return site_of((8 * grp + 2 * p) % N_QUEUE, site_id)

    left_site = site_of((window + N_QUEUE - 1) % N_QUEUE, site_id)
    right_site = site_of((window + 1) % N_QUEUE, site_id)

    lat_copy = pltpu.make_async_copy(lat_hbm, lat, lat_sem)
    lat_copy.start()
    steps_copy = pltpu.make_async_copy(steps_hbm, steps_ref, steps_sem)
    steps_copy.start()
    noise_copy = pltpu.make_async_copy(noise_hbm, next_ref.at[0], noise_sem)

    @pl.when(q == 0)
    def _():
        noise_copy.start()

    barrier = pltpu.get_barrier_semaphore()

    def greet(device):
        pl.semaphore_signal(barrier, inc=1, device_id=device, device_id_type=MESH)

    @pl.loop(0, SHARES)
    def _(i):
        greet((far, i))

    @pl.when(has_left)
    def _():
        greet(left_site)

    @pl.when(has_right)
    def _():
        greet(right_site)

    @pl.when(last)
    def _():
        for p in range(3):
            greet(relay_up(group, p))
            greet(relay_down(group + 1, p + 1))

    @pl.when(first)
    def _():
        for p in range(3):
            greet(relay_down(group, p + 1))
            greet(relay_up(group + 3, p))

    @pl.when(is_relay)
    def _():
        greet(relay_from)
        greet(relay_to)

    @pl.when(q > 0)
    def _():
        greet((q - 1, h))

    @pl.when(q < N_QUEUE - 1)
    def _():
        greet((q + 1, h))
        greet((N_QUEUE - 1, h))

    @pl.when(q == N_QUEUE - 1)
    def _():
        @pl.loop(0, N_QUEUE - 1)
        def _(i):
            greet((i, h))

    edges = SHARES + has_left.astype(jnp.int32) + has_right.astype(jnp.int32)
    edges = edges + 6 * last.astype(jnp.int32) + 6 * first.astype(jnp.int32) + 2 * is_relay.astype(jnp.int32)
    edges = edges + (q > 0).astype(jnp.int32) + 2 * (q < N_QUEUE - 1).astype(jnp.int32)
    edges = edges + (N_QUEUE - 1) * (q == N_QUEUE - 1).astype(jnp.int32)
    pl.semaphore_wait(barrier, edges)

    def scatter(src, dst, send, recv, j, row0):
        @pl.loop(0, SHARES)
        def _(n):
            i = (2 * y + n) % SHARES
            column = pl.multiple_of((i * CLASSES + j) * HEAD_DIM, HEAD_DIM)
            row = pl.multiple_of(row0 + h * ROWS, 16)
            pltpu.make_async_remote_copy(
                src_ref=src.at[:, pl.ds(column, HEAD_DIM)],
                dst_ref=dst.at[j, pl.ds(row, ROWS), :],
                send_sem=send,
                recv_sem=recv,
                device_id=site_of(q, i),
                device_id_type=MESH,
            ).start()

    def scatter_keys(j):
        scatter(k_hbm, kbuf, send_k, recv_k.at[j], j, WINDOW)

    def scatter_values(j):
        scatter(v_hbm, vbuf, send_v, recv_v.at[j], j, WINDOW)

    def scatter_queries(j):
        scatter(q_hbm, qbuf, send_q, recv_q.at[j, y], j, 0)

    def await_recv(ref, sem):
        pltpu.make_async_copy(ref, ref, sem).wait()

    def own(buf, j):
        return buf.at[j, pl.ds(WINDOW, WINDOW), :]

    def pass_on(n, buf, j, side, device, base, start, rows):
        return pltpu.make_async_remote_copy(
            src_ref=buf.at[j, pl.ds(WINDOW + start, rows), :],
            dst_ref=buf.at[j, pl.ds(base + start, rows), :],
            send_sem=send_n.at[n, side, j],
            recv_sem=recv_n.at[n, side, j],
            device_id=device,
            device_id_type=MESH,
        )

    def by_relay(n, buf, j, side, device, start):
        return pltpu.make_async_remote_copy(
            src_ref=buf.at[j, pl.ds(WINDOW + start, PIECE), :],
            dst_ref=relayed.at[n, j],
            send_sem=send_n.at[n, side, j],
            recv_sem=recv_r.at[n, j],
            device_id=device,
            device_id_type=MESH,
        )

    def forward(n, j):
        buf, recv = ((kbuf, recv_k), (vbuf, recv_v))[n]
        await_recv(own(buf, j), recv.at[j])

        @pl.when(plain_right)
        def _():
            pass_on(n, buf, j, 0, right_site, 0, 0, WINDOW).start()

        @pl.when(plain_left)
        def _():
            pass_on(n, buf, j, 1, left_site, 2 * WINDOW, 0, WINDOW).start()

        @pl.when(last)
        def _():
            pass_on(n, buf, j, 0, right_site, 0, 3 * PIECE, PIECE).start()
            for p in range(3):
                by_relay(n, buf, j, 0, relay_up(group, p), p * PIECE).start()

        @pl.when(first)
        def _():
            pass_on(n, buf, j, 1, left_site, 2 * WINDOW, 0, PIECE).start()
            for p in range(3):
                by_relay(n, buf, j, 1, relay_down(group, p + 1), (p + 1) * PIECE).start()

    def relay(j):
        @pl.when(is_relay)
        def _():
            side = jnp.where(up, 0, 1)
            row = pl.multiple_of(jnp.where(up, 0, 2 * WINDOW) + place // 2 * PIECE, 16)
            for n, buf in enumerate((kbuf, vbuf)):
                await_recv(relayed.at[n, j], recv_r.at[n, j])
                pltpu.make_async_remote_copy(
                    src_ref=relayed.at[n, j],
                    dst_ref=buf.at[j, pl.ds(row, PIECE), :],
                    send_sem=send_r.at[n, j],
                    recv_sem=recv_n.at[n, side, j],
                    device_id=relay_to,
                    device_id_type=MESH,
                ).start()

    left_flag = has_left.astype(jnp.float32)
    right_flag = has_right.astype(jnp.float32)

    def gather_context(j):
        @pl.when(has_left)
        def _():
            await_recv(kbuf.at[j, pl.ds(0, WINDOW), :], recv_n.at[0, 0, j])
            await_recv(vbuf.at[j, pl.ds(0, WINDOW), :], recv_n.at[1, 0, j])

        @pl.when(jnp.logical_not(has_left))
        def _():
            kbuf[j, 0:WINDOW, :] = kbuf[j, WINDOW:2 * WINDOW, :]
            vbuf[j, 0:WINDOW, :] = jnp.zeros((WINDOW, HEAD_DIM), jnp.bfloat16)

        @pl.when(has_right)
        def _():
            await_recv(kbuf.at[j, pl.ds(2 * WINDOW, WINDOW), :], recv_n.at[0, 1, j])
            await_recv(vbuf.at[j, pl.ds(2 * WINDOW, WINDOW), :], recv_n.at[1, 1, j])

        @pl.when(jnp.logical_not(has_right))
        def _():
            kbuf[j, 2 * WINDOW:, :] = kbuf[j, WINDOW:2 * WINDOW, :]
            vbuf[j, 2 * WINDOW:, :] = jnp.zeros((WINDOW, HEAD_DIM), jnp.bfloat16)

    def attend(j):
        @pl.loop(0, WINDOW // CHUNK)
        def _(n):
            c = (y + n) % (WINDOW // CHUNK)
            rows = pl.ds(pl.multiple_of(c * CHUNK, CHUNK), CHUNK)
            await_recv(qbuf.at[j, rows, :], recv_q.at[j, c])
            scores = lax.dot_general(
                qbuf[j, rows, :], kbuf[j], (((1,), (1,)), ((), ())),
                preferred_element_type=jnp.float32,
            )
            top = jnp.max(scores, axis=1, keepdims=True)
            weights = jnp.exp2((scores - top) * SCALE)
            total = (
                left_flag * jnp.sum(weights[:, :WINDOW], axis=1, keepdims=True)
                + jnp.sum(weights[:, WINDOW:2 * WINDOW], axis=1, keepdims=True)
                + right_flag * jnp.sum(weights[:, 2 * WINDOW:], axis=1, keepdims=True)
            )
            mixed = jnp.dot(
                weights.astype(jnp.bfloat16), vbuf[j], preferred_element_type=jnp.float32
            )
            obuf[j, rows, :] = (mixed / total).astype(jnp.bfloat16)

            for i in range(CHUNK // ROWS):
                give_back(j, c * (CHUNK // ROWS) + i)

    def give_back(j, i):
        column = pl.multiple_of(site_id * HEAD_DIM, HEAD_DIM)
        row = pl.multiple_of(i * ROWS, 16)
        pltpu.make_async_remote_copy(
            src_ref=obuf.at[j, pl.ds(row, ROWS), :],
            dst_ref=vel.at[j, :, pl.ds(column, HEAD_DIM)],
            send_sem=send_o.at[j],
            recv_sem=recv_o.at[j],
            device_id=(far, i),
            device_id_type=MESH,
        ).start()

    def levels():
        now, change = [], []
        for f in range(FRAMES):
            step = jnp.full((TOKENS, HEAD_DIM), steps_ref[f], jnp.int32)
            level = noise_level(step.astype(jnp.float32))
            level_next = noise_level((step + 1).astype(jnp.float32))
            now.append(level)
            change.append(level_next - level)
        return now, change

    def update(j):
        await_recv(obuf.at[j], recv_o.at[j])
        now, change = levels()
        for i in range(SHARES):
            head = slice((i * CLASSES + j) * HEAD_DIM, (i * CLASSES + j + 1) * HEAD_DIM)
            block = slice(i * HEAD_DIM, (i + 1) * HEAD_DIM)
            speed = vel[j, :, block].astype(jnp.float32)
            latent = lat[:, head].astype(jnp.float32)
            for f in range(FRAMES):
                frame = slice(f * TOKENS, (f + 1) * TOKENS)
                updated = (latent[frame] + change[f] * speed[frame]).astype(jnp.bfloat16)
                den_ref[f, :, head] = (latent[frame] - now[f] * speed[frame]).astype(jnp.bfloat16)
                if f < FRAMES - 1:
                    next_ref[f + 1, :, head] = updated
                else:
                    leave[j, 0:TOKENS, block] = updated

        @pl.when(q < N_QUEUE - 1)
        def _():
            frame_copy(j).start()

    def frame_copy(j):
        return pltpu.make_async_remote_copy(
            src_ref=leave.at[j],
            dst_ref=arrive.at[j],
            send_sem=send_l.at[j],
            recv_sem=recv_l.at[j],
            device_id=((q + 1) % N_QUEUE, h),
            device_id_type=MESH,
        )

    leave[:, TOKENS:, :] = jnp.zeros((CLASSES, PAD - TOKENS, SHARES * HEAD_DIM), jnp.bfloat16)

    scatter_keys(0)
    scatter_values(0)
    scatter_keys(1)
    scatter_values(1)
    forward(0, 0)
    scatter_queries(0)
    forward(1, 0)
    scatter_keys(2)
    relay(0)
    forward(0, 1)
    scatter_values(2)
    forward(1, 1)
    scatter_queries(1)
    relay(1)
    scatter_queries(2)
    gather_context(0)
    attend(0)
    forward(0, 2)
    forward(1, 2)
    relay(2)
    gather_context(1)
    attend(1)
    lat_copy.wait()
    steps_copy.wait()
    update(0)
    gather_context(2)
    attend(2)
    update(1)
    update(2)

    def fin_copy(i):
        return pltpu.make_async_remote_copy(
            src_ref=fin_stage.at[i],
            dst_ref=fin_land,
            send_sem=send_f,
            recv_sem=recv_f,
            device_id=(i, h),
            device_id_type=MESH,
        )

    @pl.when(q == N_QUEUE - 1)
    def _():
        fin_stage[:, TOKENS:, :] = jnp.zeros((N_QUEUE, PAD - TOKENS, HEAD_DIM), jnp.bfloat16)
        for i in range(SHARES):
            block = slice(i * HEAD_DIM, (i + 1) * HEAD_DIM)
            wide = jnp.concatenate(
                [leave[j, 0:TOKENS, block].astype(jnp.float32) for j in range(CLASSES)], axis=1
            )
            for p in range(4):
                piece = wide[:, p * COLUMNS:(p + 1) * COLUMNS].astype(jnp.bfloat16)
                fin_stage[4 * i + p, 0:TOKENS, 0:COLUMNS] = piece
                fin_stage[4 * i + p, 0:TOKENS, COLUMNS:] = jnp.zeros(
                    (TOKENS, HEAD_DIM - COLUMNS), jnp.bfloat16
                )

        @pl.loop(0, N_QUEUE - 1)
        def _(i):
            fin_copy(i).start()

        fin_ref[...] = fin_stage[N_QUEUE - 1, 0:TOKENS, 0:COLUMNS]

    @pl.when(q == 0)
    def _():
        noise_copy.wait()

    @pl.when(q > 0)
    def _():
        for j in range(CLASSES):
            frame_copy(j).wait_recv()
            for i in range(SHARES):
                head = slice((i * CLASSES + j) * HEAD_DIM, (i * CLASSES + j + 1) * HEAD_DIM)
                next_ref[0, :, head] = arrive[j, 0:TOKENS, i * HEAD_DIM:(i + 1) * HEAD_DIM]

    @pl.when(q < N_QUEUE - 1)
    def _():
        await_recv(fin_land, recv_f)
        fin_ref[...] = fin_land[0:TOKENS, 0:COLUMNS]

    await_recv(q_hbm, send_q)
    await_recv(k_hbm, send_k)
    await_recv(v_hbm, send_v)
    for j in range(CLASSES):
        await_recv(obuf.at[j], send_o.at[j])

        @pl.when(has_right)
        def _():
            await_recv(own(kbuf, j), send_n.at[0, 0, j])
            await_recv(own(vbuf, j), send_n.at[1, 0, j])

        @pl.when(has_left)
        def _():
            await_recv(own(kbuf, j), send_n.at[0, 1, j])
            await_recv(own(vbuf, j), send_n.at[1, 1, j])

        @pl.when(is_relay)
        def _():
            await_recv(relayed.at[0, j], send_r.at[0, j])
            await_recv(relayed.at[1, j], send_r.at[1, j])

        @pl.when(q < N_QUEUE - 1)
        def _():
            frame_copy(j).wait_send()

    @pl.when(q == N_QUEUE - 1)
    def _():
        await_recv(fin_stage.at[pl.ds(0, N_QUEUE - 1)], send_f)


def shards(latents, queries, key_proj, values, slot_steps, noise_frame):
    def flat(array):
        return array.reshape(ROWS, D)

    hbm = pl.BlockSpec(memory_space=pltpu.HBM)
    vmem = pl.BlockSpec(memory_space=pltpu.VMEM)
    bf16 = jnp.bfloat16
    dma = pltpu.SemaphoreType.DMA
    return pl.pallas_call(
        kernel,
        out_shape=(
            jax.ShapeDtypeStruct((FRAMES, TOKENS, D), bf16),
            jax.ShapeDtypeStruct((FRAMES, TOKENS, D), bf16),
            jax.ShapeDtypeStruct((TOKENS, COLUMNS), bf16),
        ),
        in_specs=[hbm] * 6,
        out_specs=(vmem, vmem, vmem),
        scratch_shapes=[
            pltpu.VMEM((CLASSES, WINDOW, HEAD_DIM), bf16),
            pltpu.VMEM((CLASSES, CONTEXT, HEAD_DIM), bf16),
            pltpu.VMEM((CLASSES, CONTEXT, HEAD_DIM), bf16),
            pltpu.VMEM((CLASSES, WINDOW, HEAD_DIM), bf16),
            pltpu.VMEM((CLASSES, ROWS, SHARES * HEAD_DIM), bf16),
            pltpu.VMEM((ROWS, D), bf16),
            pltpu.VMEM((CLASSES, PAD, SHARES * HEAD_DIM), bf16),
            pltpu.VMEM((CLASSES, PAD, SHARES * HEAD_DIM), bf16),
            pltpu.VMEM((N_QUEUE, PAD, HEAD_DIM), bf16),
            pltpu.VMEM((PAD, HEAD_DIM), bf16),
            pltpu.VMEM((2, CLASSES, PIECE, HEAD_DIM), bf16),
            pltpu.SMEM((FRAMES,), jnp.int32),
            dma, dma, dma,
            dma((CLASSES, WINDOW // CHUNK)), dma((CLASSES,)), dma((CLASSES,)),
            dma((2, 2, CLASSES)), dma((2, 2, CLASSES)), dma((2, CLASSES)), dma((2, CLASSES)),
            dma((CLASSES,)), dma((CLASSES,)),
            dma((CLASSES,)), dma((CLASSES,)),
            dma, dma, dma, dma, dma,
        ],
        compiler_params=pltpu.CompilerParams(
            collective_id=0, has_side_effects=True, vmem_limit_bytes=48 * 1024 * 1024
        ),
    )(*(pltpu.with_memory_space_constraint(a, pltpu.HBM) for a in (flat(queries), flat(key_proj), flat(values), flat(latents), noise_frame, slot_steps)))


def solution(mesh):
    spec = P("queue", "head", None)
    return jax.shard_map(
        shards,
        mesh=mesh,
        in_specs=(spec, spec, spec, spec, P("queue"), P("head", None)),
        out_specs=(spec, spec, P("head", "queue")),
        check_vma=False,
    )
```

```python
import functools
import math

import jax
import jax.numpy as jnp
from jax import lax
from jax.experimental import pallas as pl
from jax.experimental.pallas import tpu as pltpu
from jax.sharding import PartitionSpec as P

MESH = pl.DeviceIdType.MESH
HEADS = 24
HEAD_DIM = 128
D = HEADS * HEAD_DIM
FRAMES = 4
TOKENS = 24
ROWS = FRAMES * TOKENS
SHARES = 8
CLASSES = 3
WINDOW = ROWS * SHARES
CONTEXT = 3 * WINDOW
N_QUEUE = 32
STEPS = 128
HALF = N_QUEUE // 2
CHUNK = 192
PIECE = WINDOW // 4
PAD = 32
REST = ROWS - PAD
LAST = CLASSES - 1
AHEAD = SHARES * PAD
COLUMNS = D // N_QUEUE
SCALE = math.log2(math.e) / math.sqrt(HEAD_DIM)
shift_factor = 3.0


def noise_level(step_index):
    fraction = 1.0 - step_index / float(STEPS)
    return shift_factor * fraction / (1.0 + (shift_factor - 1.0) * fraction)


def kernel(
    q_hbm, k_hbm, v_hbm, lat_hbm, noise_hbm, steps_hbm,
    next_ref, den_ref, fin_ref,
    qbuf, kbuf, vbuf, obuf, vel, lat, leave, arrive, fin_stage, fin_land, relayed, steps_ref,
    send_q, send_k, send_v, recv_q, recv_k, recv_v,
    send_n, recv_n, send_r, recv_r,
    send_o, recv_o, send_l, recv_l, send_f, recv_f, lat_sem, noise_sem, steps_sem,
):
    q = lax.axis_index("queue")
    h = lax.axis_index("head")
    y, z_hi = h // 2, h % 2
    z_lo = q // 8
    far = (q + HALF) % N_QUEUE

    def flip(window):
        return (window // 16) % 2

    s_mine = (z_hi + flip(far)) % 2
    site_id = y * 2 + s_mine
    window = far

    def site_of(win, ident):
        return ((win + HALF) % N_QUEUE, (ident // 2) * 2 + (ident + flip(win)) % 2)

    group, place = window // 8, window % 8
    has_left = window > 0
    has_right = window < N_QUEUE - 1
    last = jnp.logical_and(place == 7, has_right)
    first = jnp.logical_and(place == 0, has_left)
    plain_right = place < 7
    plain_left = place > 0
    up = jnp.logical_and(jnp.logical_and(place % 2 == 1, place < 7), group < 3)
    down = jnp.logical_and(jnp.logical_and(place % 2 == 0, place > 0), group > 0)
    is_relay = jnp.logical_or(up, down)
    relay_from = site_of(jnp.where(up, 8 * group + 7, 8 * group), site_id)
    relay_to = site_of(jnp.where(up, 8 * group + 8, (8 * group + N_QUEUE - 1) % N_QUEUE) % N_QUEUE, site_id)

    def relay_up(grp, p):
        return site_of((8 * grp + 2 * p + 1) % N_QUEUE, site_id)

    def relay_down(grp, p):
        return site_of((8 * grp + 2 * p) % N_QUEUE, site_id)

    left_site = site_of((window + N_QUEUE - 1) % N_QUEUE, site_id)
    right_site = site_of((window + 1) % N_QUEUE, site_id)

    lat_copy = pltpu.make_async_copy(lat_hbm, lat, lat_sem)
    lat_copy.start()
    steps_copy = pltpu.make_async_copy(steps_hbm, steps_ref, steps_sem)
    steps_copy.start()
    noise_copy = pltpu.make_async_copy(noise_hbm, next_ref.at[0], noise_sem)

    @pl.when(q == 0)
    def _():
        noise_copy.start()

    barrier = pltpu.get_barrier_semaphore()

    def greet(device):
        pl.semaphore_signal(barrier, inc=1, device_id=device, device_id_type=MESH)

    @pl.loop(0, SHARES)
    def _(i):
        greet((far, i))

    @pl.when(has_left)
    def _():
        greet(left_site)

    @pl.when(has_right)
    def _():
        greet(right_site)

    @pl.when(last)
    def _():
        for p in range(3):
            greet(relay_up(group, p))
            greet(relay_down(group + 1, p + 1))

    @pl.when(first)
    def _():
        for p in range(3):
            greet(relay_down(group, p + 1))
            greet(relay_up(group + 3, p))

    @pl.when(is_relay)
    def _():
        greet(relay_from)
        greet(relay_to)

    @pl.when(q > 0)
    def _():
        greet((q - 1, h))

    @pl.when(q < N_QUEUE - 1)
    def _():
        greet((q + 1, h))
        greet((N_QUEUE - 1, h))

    @pl.when(q == N_QUEUE - 1)
    def _():
        @pl.loop(0, N_QUEUE - 1)
        def _(i):
            greet((i, h))

    edges = SHARES + has_left.astype(jnp.int32) + has_right.astype(jnp.int32)
    edges = edges + 6 * last.astype(jnp.int32) + 6 * first.astype(jnp.int32) + 2 * is_relay.astype(jnp.int32)
    edges = edges + (q > 0).astype(jnp.int32) + 2 * (q < N_QUEUE - 1).astype(jnp.int32)
    edges = edges + (N_QUEUE - 1) * (q == N_QUEUE - 1).astype(jnp.int32)
    pl.semaphore_wait(barrier, edges)

    def scatter(src, dst, send, recv, j, row0):
        @pl.loop(0, SHARES)
        def _(n):
            i = (2 * y + n) % SHARES
            column = pl.multiple_of((i * CLASSES + j) * HEAD_DIM, HEAD_DIM)
            row = pl.multiple_of(row0 + h * ROWS, 16)
            pltpu.make_async_remote_copy(
                src_ref=src.at[:, pl.ds(column, HEAD_DIM)],
                dst_ref=dst.at[j, pl.ds(row, ROWS), :],
                send_sem=send,
                recv_sem=recv,
                device_id=site_of(q, i),
                device_id_type=MESH,
            ).start()

    def scatter_keys(j):
        scatter(k_hbm, kbuf, send_k, recv_k.at[j], j, WINDOW)

    def scatter_values(j):
        scatter(v_hbm, vbuf, send_v, recv_v.at[j], j, WINDOW)

    def scatter_queries(j):
        if j < LAST:
            scatter(q_hbm, qbuf, send_q, recv_q.at[j, y], j, 0)
            return
        for rows, start, place_of, sem in (
            (PAD, REST, h * PAD, recv_q.at[j, 0]),
            (REST, 0, AHEAD + h * REST, recv_q.at[j, 1 + h // 4]),
        ):
            @pl.loop(0, SHARES)
            def _(n):
                i = (2 * y + n) % SHARES
                column = pl.multiple_of((i * CLASSES + j) * HEAD_DIM, HEAD_DIM)
                pltpu.make_async_remote_copy(
                    src_ref=q_hbm.at[pl.ds(start, rows), pl.ds(column, HEAD_DIM)],
                    dst_ref=qbuf.at[j, pl.ds(pl.multiple_of(place_of, 16), rows), :],
                    send_sem=send_q,
                    recv_sem=sem,
                    device_id=site_of(q, i),
                    device_id_type=MESH,
                ).start()

    def await_recv(ref, sem):
        pltpu.make_async_copy(ref, ref, sem).wait()

    def own(buf, j):
        return buf.at[j, pl.ds(WINDOW, WINDOW), :]

    def pass_on(n, buf, j, side, device, base, start, rows):
        return pltpu.make_async_remote_copy(
            src_ref=buf.at[j, pl.ds(WINDOW + start, rows), :],
            dst_ref=buf.at[j, pl.ds(base + start, rows), :],
            send_sem=send_n.at[n, side, j],
            recv_sem=recv_n.at[n, side, j],
            device_id=device,
            device_id_type=MESH,
        )

    def by_relay(n, buf, j, side, device, start):
        return pltpu.make_async_remote_copy(
            src_ref=buf.at[j, pl.ds(WINDOW + start, PIECE), :],
            dst_ref=relayed.at[n, j],
            send_sem=send_n.at[n, side, j],
            recv_sem=recv_r.at[n, j],
            device_id=device,
            device_id_type=MESH,
        )

    def forward(n, j):
        buf, recv = ((kbuf, recv_k), (vbuf, recv_v))[n]
        await_recv(own(buf, j), recv.at[j])

        @pl.when(plain_right)
        def _():
            pass_on(n, buf, j, 0, right_site, 0, 0, WINDOW).start()

        @pl.when(plain_left)
        def _():
            pass_on(n, buf, j, 1, left_site, 2 * WINDOW, 0, WINDOW).start()

        @pl.when(last)
        def _():
            pass_on(n, buf, j, 0, right_site, 0, 3 * PIECE, PIECE).start()
            for p in range(3):
                by_relay(n, buf, j, 0, relay_up(group, p), p * PIECE).start()

        @pl.when(first)
        def _():
            pass_on(n, buf, j, 1, left_site, 2 * WINDOW, 0, PIECE).start()
            for p in range(3):
                by_relay(n, buf, j, 1, relay_down(group, p + 1), (p + 1) * PIECE).start()

    def relay(n, j):
        buf = (kbuf, vbuf)[n]

        @pl.when(is_relay)
        def _():
            side = jnp.where(up, 0, 1)
            row = pl.multiple_of(jnp.where(up, 0, 2 * WINDOW) + place // 2 * PIECE, 16)
            await_recv(relayed.at[n, j], recv_r.at[n, j])
            pltpu.make_async_remote_copy(
                src_ref=relayed.at[n, j],
                dst_ref=buf.at[j, pl.ds(row, PIECE), :],
                send_sem=send_r.at[n, j],
                recv_sem=recv_n.at[n, side, j],
                device_id=relay_to,
                device_id_type=MESH,
            ).start()

    left_flag = has_left.astype(jnp.float32)
    right_flag = has_right.astype(jnp.float32)

    def gather_context(j):
        @pl.when(has_left)
        def _():
            await_recv(kbuf.at[j, pl.ds(0, WINDOW), :], recv_n.at[0, 0, j])
            await_recv(vbuf.at[j, pl.ds(0, WINDOW), :], recv_n.at[1, 0, j])

        @pl.when(jnp.logical_not(has_left))
        def _():
            kbuf[j, 0:WINDOW, :] = kbuf[j, WINDOW:2 * WINDOW, :]
            vbuf[j, 0:WINDOW, :] = jnp.zeros((WINDOW, HEAD_DIM), jnp.bfloat16)

        @pl.when(has_right)
        def _():
            await_recv(kbuf.at[j, pl.ds(2 * WINDOW, WINDOW), :], recv_n.at[0, 1, j])
            await_recv(vbuf.at[j, pl.ds(2 * WINDOW, WINDOW), :], recv_n.at[1, 1, j])

        @pl.when(jnp.logical_not(has_right))
        def _():
            kbuf[j, 2 * WINDOW:, :] = kbuf[j, WINDOW:2 * WINDOW, :]
            vbuf[j, 2 * WINDOW:, :] = jnp.zeros((WINDOW, HEAD_DIM), jnp.bfloat16)

    def attend_rows(j, rows):
        scores = lax.dot_general(
            qbuf[j, rows, :], kbuf[j], (((1,), (1,)), ((), ())),
            preferred_element_type=jnp.float32,
        )
        top = jnp.max(scores, axis=1, keepdims=True)
        weights = jnp.exp2((scores - top) * SCALE)
        total = (
            left_flag * jnp.sum(weights[:, :WINDOW], axis=1, keepdims=True)
            + jnp.sum(weights[:, WINDOW:2 * WINDOW], axis=1, keepdims=True)
            + right_flag * jnp.sum(weights[:, 2 * WINDOW:], axis=1, keepdims=True)
        )
        mixed = jnp.dot(
            weights.astype(jnp.bfloat16), vbuf[j], preferred_element_type=jnp.float32
        )
        obuf[j, rows, :] = (mixed / total).astype(jnp.bfloat16)

    def attend(j):
        if j < LAST:
            @pl.loop(0, WINDOW // CHUNK)
            def _(n):
                c = (y + n) % (WINDOW // CHUNK)
                rows = pl.ds(pl.multiple_of(c * CHUNK, CHUNK), CHUNK)
                await_recv(qbuf.at[j, rows, :], recv_q.at[j, c])
                attend_rows(j, rows)
                for i in range(CHUNK // ROWS):
                    share = c * (CHUNK // ROWS) + i
                    give_back(j, share, pl.multiple_of(share * ROWS, 16), 0, ROWS, 0)
            return

        ahead = pl.ds(0, AHEAD)
        await_recv(qbuf.at[j, ahead, :], recv_q.at[j, 0])
        attend_rows(j, ahead)

        @pl.loop(0, SHARES)
        def _(n):
            share = (2 * y + n) % SHARES
            give_back(j, share, pl.multiple_of(share * PAD, 16), REST, PAD, 0)

        @pl.loop(0, 2)
        def _(n):
            c = (y // 2 + n) % 2
            rows = pl.ds(pl.multiple_of(AHEAD + c * 4 * REST, 16), 4 * REST)
            await_recv(qbuf.at[j, rows, :], recv_q.at[j, 1 + c])
            attend_rows(j, rows)
            for i in range(4):
                share = 4 * c + i
                give_back(j, share, pl.multiple_of(AHEAD + share * REST, 16), 0, REST, 1)

    def give_back(j, share, row, start, rows, part):
        column = pl.multiple_of(site_id * HEAD_DIM, HEAD_DIM)
        pltpu.make_async_remote_copy(
            src_ref=obuf.at[j, pl.ds(row, rows), :],
            dst_ref=vel.at[j, pl.ds(start, rows), pl.ds(column, HEAD_DIM)],
            send_sem=send_o.at[j],
            recv_sem=recv_o.at[j + part],
            device_id=(far, share),
            device_id_type=MESH,
        ).start()

    def levels():
        now, change = [], []
        for f in range(FRAMES):
            step = jnp.full((TOKENS, HEAD_DIM), steps_ref[f], jnp.int32)
            level = noise_level(step.astype(jnp.float32))
            level_next = noise_level((step + 1).astype(jnp.float32))
            now.append(level)
            change.append(level_next - level)
        return now, change

    def update(j, frames):
        now, change = levels()
        for i in range(SHARES):
            head = slice((i * CLASSES + j) * HEAD_DIM, (i * CLASSES + j + 1) * HEAD_DIM)
            block = slice(i * HEAD_DIM, (i + 1) * HEAD_DIM)
            base = REST if min(frames) == FRAMES - 1 else 0
            speed = vel[j, base:, block].astype(jnp.float32)
            latent = lat[base:, head].astype(jnp.float32)
            for f in frames:
                frame = slice(f * TOKENS - base, (f + 1) * TOKENS - base)
                updated = (latent[frame] + change[f] * speed[frame]).astype(jnp.bfloat16)
                den_ref[f, :, head] = (latent[frame] - now[f] * speed[frame]).astype(jnp.bfloat16)
                if f < FRAMES - 1:
                    next_ref[f + 1, :, head] = updated
                else:
                    leave[j, 0:TOKENS, block] = updated

        if FRAMES - 1 in frames:
            @pl.when(q < N_QUEUE - 1)
            def _():
                frame_copy(j).start()

    def update_whole(j):
        await_recv(obuf.at[j], recv_o.at[j])
        update(j, range(FRAMES))

    def update_ahead():
        await_recv(obuf.at[LAST, pl.ds(0, AHEAD), :], recv_o.at[LAST])
        update(LAST, (FRAMES - 1,))

    def update_rest():
        await_recv(obuf.at[LAST, pl.ds(AHEAD, WINDOW - AHEAD), :], recv_o.at[LAST + 1])
        update(LAST, range(FRAMES - 1))

    def frame_copy(j):
        return pltpu.make_async_remote_copy(
            src_ref=leave.at[j],
            dst_ref=arrive.at[j],
            send_sem=send_l.at[j],
            recv_sem=recv_l.at[j],
            device_id=((q + 1) % N_QUEUE, h),
            device_id_type=MESH,
        )

    leave[:, TOKENS:, :] = jnp.zeros((CLASSES, PAD - TOKENS, SHARES * HEAD_DIM), jnp.bfloat16)

    scatter_keys(0)
    scatter_values(0)
    scatter_keys(1)
    scatter_values(1)
    forward(0, 0)
    scatter_queries(0)
    forward(1, 0)
    scatter_keys(2)
    relay(0, 0)
    relay(1, 0)
    forward(0, 1)
    scatter_values(2)
    relay(0, 1)
    forward(1, 1)
    scatter_queries(1)
    relay(1, 1)
    gather_context(0)
    attend(0)
    forward(0, 2)
    relay(0, 2)
    forward(1, 2)
    scatter_queries(2)
    relay(1, 2)
    gather_context(1)
    attend(1)
    lat_copy.wait()
    steps_copy.wait()
    update_whole(0)
    gather_context(2)
    attend(2)
    update_whole(1)

    update_ahead()

    def fin_copy(i):
        return pltpu.make_async_remote_copy(
            src_ref=fin_stage.at[i],
            dst_ref=fin_land,
            send_sem=send_f,
            recv_sem=recv_f,
            device_id=(i, h),
            device_id_type=MESH,
        )

    @pl.when(q == N_QUEUE - 1)
    def _():
        fin_stage[:, TOKENS:, :] = jnp.zeros((N_QUEUE, PAD - TOKENS, HEAD_DIM), jnp.bfloat16)
        for i in range(SHARES):
            block = slice(i * HEAD_DIM, (i + 1) * HEAD_DIM)
            wide = jnp.concatenate(
                [leave[j, 0:TOKENS, block].astype(jnp.float32) for j in range(CLASSES)], axis=1
            )
            for p in range(4):
                piece = wide[:, p * COLUMNS:(p + 1) * COLUMNS].astype(jnp.bfloat16)
                fin_stage[4 * i + p, 0:TOKENS, 0:COLUMNS] = piece
                fin_stage[4 * i + p, 0:TOKENS, COLUMNS:] = jnp.zeros(
                    (TOKENS, HEAD_DIM - COLUMNS), jnp.bfloat16
                )

        @pl.loop(0, N_QUEUE - 1)
        def _(i):
            fin_copy(i).start()

        fin_ref[...] = fin_stage[N_QUEUE - 1, 0:TOKENS, 0:COLUMNS]

    update_rest()

    @pl.when(q == 0)
    def _():
        noise_copy.wait()

    @pl.when(q > 0)
    def _():
        for j in range(CLASSES):
            frame_copy(j).wait_recv()
            for i in range(SHARES):
                head = slice((i * CLASSES + j) * HEAD_DIM, (i * CLASSES + j + 1) * HEAD_DIM)
                next_ref[0, :, head] = arrive[j, 0:TOKENS, i * HEAD_DIM:(i + 1) * HEAD_DIM]

    @pl.when(q < N_QUEUE - 1)
    def _():
        await_recv(fin_land, recv_f)
        fin_ref[...] = fin_land[0:TOKENS, 0:COLUMNS]

    await_recv(q_hbm, send_q)
    await_recv(k_hbm, send_k)
    await_recv(v_hbm, send_v)
    for j in range(CLASSES):
        await_recv(obuf.at[j], send_o.at[j])

        @pl.when(has_right)
        def _():
            await_recv(own(kbuf, j), send_n.at[0, 0, j])
            await_recv(own(vbuf, j), send_n.at[1, 0, j])

        @pl.when(has_left)
        def _():
            await_recv(own(kbuf, j), send_n.at[0, 1, j])
            await_recv(own(vbuf, j), send_n.at[1, 1, j])

        @pl.when(is_relay)
        def _():
            await_recv(relayed.at[0, j], send_r.at[0, j])
            await_recv(relayed.at[1, j], send_r.at[1, j])

        @pl.when(q < N_QUEUE - 1)
        def _():
            frame_copy(j).wait_send()

    @pl.when(q == N_QUEUE - 1)
    def _():
        await_recv(fin_stage.at[pl.ds(0, N_QUEUE - 1)], send_f)


def shards(latents, queries, key_proj, values, slot_steps, noise_frame):
    def flat(array):
        return array.reshape(ROWS, D)

    hbm = pl.BlockSpec(memory_space=pltpu.HBM)
    vmem = pl.BlockSpec(memory_space=pltpu.VMEM)
    bf16 = jnp.bfloat16
    dma = pltpu.SemaphoreType.DMA
    return pl.pallas_call(
        kernel,
        out_shape=(
            jax.ShapeDtypeStruct((FRAMES, TOKENS, D), bf16),
            jax.ShapeDtypeStruct((FRAMES, TOKENS, D), bf16),
            jax.ShapeDtypeStruct((TOKENS, COLUMNS), bf16),
        ),
        in_specs=[hbm] * 6,
        out_specs=(vmem, vmem, vmem),
        scratch_shapes=[
            pltpu.VMEM((CLASSES, WINDOW, HEAD_DIM), bf16),
            pltpu.VMEM((CLASSES, CONTEXT, HEAD_DIM), bf16),
            pltpu.VMEM((CLASSES, CONTEXT, HEAD_DIM), bf16),
            pltpu.VMEM((CLASSES, WINDOW, HEAD_DIM), bf16),
            pltpu.VMEM((CLASSES, ROWS, SHARES * HEAD_DIM), bf16),
            pltpu.VMEM((ROWS, D), bf16),
            pltpu.VMEM((CLASSES, PAD, SHARES * HEAD_DIM), bf16),
            pltpu.VMEM((CLASSES, PAD, SHARES * HEAD_DIM), bf16),
            pltpu.VMEM((N_QUEUE, PAD, HEAD_DIM), bf16),
            pltpu.VMEM((PAD, HEAD_DIM), bf16),
            pltpu.VMEM((2, CLASSES, PIECE, HEAD_DIM), bf16),
            pltpu.SMEM((FRAMES,), jnp.int32),
            dma, dma, dma,
            dma((CLASSES, WINDOW // CHUNK)), dma((CLASSES,)), dma((CLASSES,)),
            dma((2, 2, CLASSES)), dma((2, 2, CLASSES)), dma((2, CLASSES)), dma((2, CLASSES)),
            dma((CLASSES,)), dma((CLASSES + 1,)),
            dma((CLASSES,)), dma((CLASSES,)),
            dma, dma, dma, dma, dma,
        ],
        compiler_params=pltpu.CompilerParams(
            collective_id=0, has_side_effects=True, vmem_limit_bytes=48 * 1024 * 1024
        ),
    )(*(pltpu.with_memory_space_constraint(a, pltpu.HBM) for a in (flat(queries), flat(key_proj), flat(values), flat(latents), noise_frame, slot_steps)))


def solution(mesh):
    spec = P("queue", "head", None)
    return jax.shard_map(
        shards,
        mesh=mesh,
        in_specs=(spec, spec, spec, spec, P("queue"), P("head", None)),
        out_specs=(spec, spec, P("head", "queue")),
        check_vma=False,
    )
```

```python
import functools
import math

import jax
import jax.numpy as jnp
from jax import lax
from jax.experimental import pallas as pl
from jax.experimental.pallas import tpu as pltpu
from jax.sharding import PartitionSpec as P

MESH = pl.DeviceIdType.MESH
HEADS = 24
HEAD_DIM = 128
D = HEADS * HEAD_DIM
FRAMES = 4
TOKENS = 24
ROWS = FRAMES * TOKENS
SHARES = 8
CLASSES = 3
WINDOW = ROWS * SHARES
CONTEXT = 3 * WINDOW
N_QUEUE = 32
STEPS = 128
HALF = N_QUEUE // 2
CHUNK = 192
PIECE = WINDOW // 4
PAD = 32
REST = ROWS - PAD
LAST = CLASSES - 1
AHEAD = SHARES * PAD
COLUMNS = D // N_QUEUE
SCALE = math.log2(math.e) / math.sqrt(HEAD_DIM)
shift_factor = 3.0


def noise_level(step_index):
    fraction = 1.0 - step_index / float(STEPS)
    return shift_factor * fraction / (1.0 + (shift_factor - 1.0) * fraction)


def kernel(
    q_hbm, k_hbm, v_hbm, lat_hbm, noise_hbm, steps_hbm,
    next_ref, den_ref, fin_ref,
    qbuf, kbuf, vbuf, obuf, vel, lat, leave, arrive, fin_stage, fin_land, relayed, steps_ref,
    send_q, send_k, send_v, recv_q, recv_k, recv_v,
    send_n, recv_n, send_r, recv_r,
    send_o, recv_o, send_l, recv_l, send_f, recv_f, lat_sem, noise_sem, steps_sem,
):
    q = lax.axis_index("queue")
    h = lax.axis_index("head")
    y, z_hi = h // 2, h % 2
    z_lo = q // 8
    far = (q + HALF) % N_QUEUE

    def flip(window):
        return (window // 16) % 2

    s_mine = (z_hi + flip(far)) % 2
    site_id = y * 2 + s_mine
    window = far

    def site_of(win, ident):
        return ((win + HALF) % N_QUEUE, (ident // 2) * 2 + (ident + flip(win)) % 2)

    group, place = window // 8, window % 8
    has_left = window > 0
    has_right = window < N_QUEUE - 1
    last = jnp.logical_and(place == 7, has_right)
    first = jnp.logical_and(place == 0, has_left)
    plain_right = place < 7
    plain_left = place > 0
    up = jnp.logical_and(jnp.logical_and(place % 2 == 1, place < 7), group < 3)
    down = jnp.logical_and(jnp.logical_and(place % 2 == 0, place > 0), group > 0)
    is_relay = jnp.logical_or(up, down)
    relay_from = site_of(jnp.where(up, 8 * group + 7, 8 * group), site_id)
    relay_to = site_of(jnp.where(up, 8 * group + 8, (8 * group + N_QUEUE - 1) % N_QUEUE) % N_QUEUE, site_id)

    def relay_up(grp, p):
        return site_of((8 * grp + 2 * p + 1) % N_QUEUE, site_id)

    def relay_down(grp, p):
        return site_of((8 * grp + 2 * p) % N_QUEUE, site_id)

    left_site = site_of((window + N_QUEUE - 1) % N_QUEUE, site_id)
    right_site = site_of((window + 1) % N_QUEUE, site_id)

    lat_copy = pltpu.make_async_copy(lat_hbm, lat, lat_sem)
    lat_copy.start()
    steps_copy = pltpu.make_async_copy(steps_hbm, steps_ref, steps_sem)
    steps_copy.start()
    noise_copy = pltpu.make_async_copy(noise_hbm, next_ref.at[0], noise_sem)

    @pl.when(q == 0)
    def _():
        noise_copy.start()

    barrier = pltpu.get_barrier_semaphore()

    def greet(device):
        pl.semaphore_signal(barrier, inc=1, device_id=device, device_id_type=MESH)

    @pl.loop(0, SHARES)
    def _(i):
        greet((far, i))

    @pl.when(has_left)
    def _():
        greet(left_site)

    @pl.when(has_right)
    def _():
        greet(right_site)

    @pl.when(last)
    def _():
        for p in range(3):
            greet(relay_down(group + 1, p + 1))

    @pl.when(first)
    def _():
        for p in range(3):
            greet(relay_up(group + 3, p))

    @pl.when(is_relay)
    def _():
        greet(relay_from)

    @pl.when(q > 0)
    def _():
        greet((q - 1, h))

    @pl.when(q < N_QUEUE - 1)
    def _():
        greet((N_QUEUE - 1, h))

    edges = SHARES + has_left.astype(jnp.int32) + has_right.astype(jnp.int32)
    edges = edges + 3 * last.astype(jnp.int32) + 3 * first.astype(jnp.int32) + is_relay.astype(jnp.int32)
    edges = edges + (q < N_QUEUE - 1).astype(jnp.int32)
    edges = edges + (N_QUEUE - 1) * (q == N_QUEUE - 1).astype(jnp.int32)
    pl.semaphore_wait(barrier, edges)

    def scatter(src, dst, send, recv, j, row0):
        @pl.loop(0, SHARES)
        def _(n):
            i = (2 * y + n) % SHARES
            column = pl.multiple_of((i * CLASSES + j) * HEAD_DIM, HEAD_DIM)
            row = pl.multiple_of(row0 + h * ROWS, 16)
            pltpu.make_async_remote_copy(
                src_ref=src.at[:, pl.ds(column, HEAD_DIM)],
                dst_ref=dst.at[j, pl.ds(row, ROWS), :],
                send_sem=send,
                recv_sem=recv,
                device_id=site_of(q, i),
                device_id_type=MESH,
            ).start()

    def scatter_keys(j):
        scatter(k_hbm, kbuf, send_k, recv_k.at[j], j, WINDOW)

    def scatter_values(j):
        scatter(v_hbm, vbuf, send_v, recv_v.at[j], j, WINDOW)

    def scatter_queries(j):
        if j < LAST:
            scatter(q_hbm, qbuf, send_q, recv_q.at[j, y], j, 0)
            return
        for rows, start, place_of, sem in (
            (PAD, REST, h * PAD, recv_q.at[j, 0]),
            (REST, 0, AHEAD + h * REST, recv_q.at[j, 1 + h // 4]),
        ):
            @pl.loop(0, SHARES)
            def _(n):
                i = (2 * y + n) % SHARES
                column = pl.multiple_of((i * CLASSES + j) * HEAD_DIM, HEAD_DIM)
                pltpu.make_async_remote_copy(
                    src_ref=q_hbm.at[pl.ds(start, rows), pl.ds(column, HEAD_DIM)],
                    dst_ref=qbuf.at[j, pl.ds(pl.multiple_of(place_of, 16), rows), :],
                    send_sem=send_q,
                    recv_sem=sem,
                    device_id=site_of(q, i),
                    device_id_type=MESH,
                ).start()

    def await_recv(ref, sem):
        pltpu.make_async_copy(ref, ref, sem).wait()

    def own(buf, j):
        return buf.at[j, pl.ds(WINDOW, WINDOW), :]

    def pass_on(n, buf, j, side, device, base, start, rows):
        return pltpu.make_async_remote_copy(
            src_ref=buf.at[j, pl.ds(WINDOW + start, rows), :],
            dst_ref=buf.at[j, pl.ds(base + start, rows), :],
            send_sem=send_n.at[n, side, j],
            recv_sem=recv_n.at[n, side, j],
            device_id=device,
            device_id_type=MESH,
        )

    def by_relay(n, buf, j, side, device, start):
        return pltpu.make_async_remote_copy(
            src_ref=buf.at[j, pl.ds(WINDOW + start, PIECE), :],
            dst_ref=relayed.at[n, j],
            send_sem=send_n.at[n, side, j],
            recv_sem=recv_r.at[n, j],
            device_id=device,
            device_id_type=MESH,
        )

    def forward(n, j):
        buf, recv = ((kbuf, recv_k), (vbuf, recv_v))[n]
        await_recv(own(buf, j), recv.at[j])

        @pl.when(plain_right)
        def _():
            pass_on(n, buf, j, 0, right_site, 0, 0, WINDOW).start()

        @pl.when(plain_left)
        def _():
            pass_on(n, buf, j, 1, left_site, 2 * WINDOW, 0, WINDOW).start()

        @pl.when(last)
        def _():
            pass_on(n, buf, j, 0, right_site, 0, 3 * PIECE, PIECE).start()
            for p in range(3):
                by_relay(n, buf, j, 0, relay_up(group, p), p * PIECE).start()

        @pl.when(first)
        def _():
            pass_on(n, buf, j, 1, left_site, 2 * WINDOW, 0, PIECE).start()
            for p in range(3):
                by_relay(n, buf, j, 1, relay_down(group, p + 1), (p + 1) * PIECE).start()

    def relay(n, j):
        buf = (kbuf, vbuf)[n]

        @pl.when(is_relay)
        def _():
            side = jnp.where(up, 0, 1)
            row = pl.multiple_of(jnp.where(up, 0, 2 * WINDOW) + place // 2 * PIECE, 16)
            await_recv(relayed.at[n, j], recv_r.at[n, j])
            pltpu.make_async_remote_copy(
                src_ref=relayed.at[n, j],
                dst_ref=buf.at[j, pl.ds(row, PIECE), :],
                send_sem=send_r.at[n, j],
                recv_sem=recv_n.at[n, side, j],
                device_id=relay_to,
                device_id_type=MESH,
            ).start()

    left_flag = has_left.astype(jnp.float32)
    right_flag = has_right.astype(jnp.float32)

    def gather_context(j):
        @pl.when(has_left)
        def _():
            await_recv(kbuf.at[j, pl.ds(0, WINDOW), :], recv_n.at[0, 0, j])
            await_recv(vbuf.at[j, pl.ds(0, WINDOW), :], recv_n.at[1, 0, j])

        @pl.when(jnp.logical_not(has_left))
        def _():
            kbuf[j, 0:WINDOW, :] = kbuf[j, WINDOW:2 * WINDOW, :]
            vbuf[j, 0:WINDOW, :] = jnp.zeros((WINDOW, HEAD_DIM), jnp.bfloat16)

        @pl.when(has_right)
        def _():
            await_recv(kbuf.at[j, pl.ds(2 * WINDOW, WINDOW), :], recv_n.at[0, 1, j])
            await_recv(vbuf.at[j, pl.ds(2 * WINDOW, WINDOW), :], recv_n.at[1, 1, j])

        @pl.when(jnp.logical_not(has_right))
        def _():
            kbuf[j, 2 * WINDOW:, :] = kbuf[j, WINDOW:2 * WINDOW, :]
            vbuf[j, 2 * WINDOW:, :] = jnp.zeros((WINDOW, HEAD_DIM), jnp.bfloat16)

    def attend_rows(j, rows):
        scores = lax.dot_general(
            qbuf[j, rows, :], kbuf[j], (((1,), (1,)), ((), ())),
            preferred_element_type=jnp.float32,
        )
        top = jnp.max(scores, axis=1, keepdims=True)
        weights = jnp.exp2((scores - top) * SCALE)
        total = (
            left_flag * jnp.sum(weights[:, :WINDOW], axis=1, keepdims=True)
            + jnp.sum(weights[:, WINDOW:2 * WINDOW], axis=1, keepdims=True)
            + right_flag * jnp.sum(weights[:, 2 * WINDOW:], axis=1, keepdims=True)
        )
        mixed = jnp.dot(
            weights.astype(jnp.bfloat16), vbuf[j], preferred_element_type=jnp.float32
        )
        obuf[j, rows, :] = (mixed / total).astype(jnp.bfloat16)

    def attend(j):
        if j < LAST:
            @pl.loop(0, WINDOW // CHUNK)
            def _(n):
                c = (y + n) % (WINDOW // CHUNK)
                rows = pl.ds(pl.multiple_of(c * CHUNK, CHUNK), CHUNK)
                await_recv(qbuf.at[j, rows, :], recv_q.at[j, c])
                attend_rows(j, rows)
                for i in range(CHUNK // ROWS):
                    share = c * (CHUNK // ROWS) + i
                    give_back(j, share, pl.multiple_of(share * ROWS, 16), 0, ROWS, 0)
            return

        ahead = pl.ds(0, AHEAD)
        await_recv(qbuf.at[j, ahead, :], recv_q.at[j, 0])
        attend_rows(j, ahead)

        @pl.loop(0, SHARES)
        def _(n):
            share = (2 * y + n) % SHARES
            give_back(j, share, pl.multiple_of(share * PAD, 16), REST, PAD, 0)

        @pl.loop(0, 2)
        def _(n):
            c = (y // 2 + n) % 2
            rows = pl.ds(pl.multiple_of(AHEAD + c * 4 * REST, 16), 4 * REST)
            await_recv(qbuf.at[j, rows, :], recv_q.at[j, 1 + c])
            attend_rows(j, rows)
            for i in range(4):
                share = 4 * c + i
                give_back(j, share, pl.multiple_of(AHEAD + share * REST, 16), 0, REST, 1)

    def give_back(j, share, row, start, rows, part):
        column = pl.multiple_of(site_id * HEAD_DIM, HEAD_DIM)
        pltpu.make_async_remote_copy(
            src_ref=obuf.at[j, pl.ds(row, rows), :],
            dst_ref=vel.at[j, pl.ds(start, rows), pl.ds(column, HEAD_DIM)],
            send_sem=send_o.at[j],
            recv_sem=recv_o.at[j + part],
            device_id=(far, share),
            device_id_type=MESH,
        ).start()

    def levels():
        now, change = [], []
        for f in range(FRAMES):
            step = jnp.full((TOKENS, HEAD_DIM), steps_ref[f], jnp.int32)
            level = noise_level(step.astype(jnp.float32))
            level_next = noise_level((step + 1).astype(jnp.float32))
            now.append(level)
            change.append(level_next - level)
        return now, change

    def update(j, frames):
        now, change = levels()
        for i in range(SHARES):
            head = slice((i * CLASSES + j) * HEAD_DIM, (i * CLASSES + j + 1) * HEAD_DIM)
            block = slice(i * HEAD_DIM, (i + 1) * HEAD_DIM)
            base = REST if min(frames) == FRAMES - 1 else 0
            speed = vel[j, base:, block].astype(jnp.float32)
            latent = lat[base:, head].astype(jnp.float32)
            for f in frames:
                frame = slice(f * TOKENS - base, (f + 1) * TOKENS - base)
                updated = (latent[frame] + change[f] * speed[frame]).astype(jnp.bfloat16)
                den_ref[f, :, head] = (latent[frame] - now[f] * speed[frame]).astype(jnp.bfloat16)
                if f < FRAMES - 1:
                    next_ref[f + 1, :, head] = updated
                else:
                    leave[j, 0:TOKENS, block] = updated

        if FRAMES - 1 in frames:
            @pl.when(q < N_QUEUE - 1)
            def _():
                frame_copy(j).start()

    def update_whole(j):
        await_recv(obuf.at[j], recv_o.at[j])
        update(j, range(FRAMES))

    def update_ahead():
        await_recv(obuf.at[LAST, pl.ds(0, AHEAD), :], recv_o.at[LAST])
        update(LAST, (FRAMES - 1,))

    def update_rest():
        await_recv(obuf.at[LAST, pl.ds(AHEAD, WINDOW - AHEAD), :], recv_o.at[LAST + 1])
        update(LAST, range(FRAMES - 1))

    def frame_copy(j):
        return pltpu.make_async_remote_copy(
            src_ref=leave.at[j],
            dst_ref=arrive.at[j],
            send_sem=send_l.at[j],
            recv_sem=recv_l.at[j],
            device_id=((q + 1) % N_QUEUE, h),
            device_id_type=MESH,
        )

    leave[:, TOKENS:, :] = jnp.zeros((CLASSES, PAD - TOKENS, SHARES * HEAD_DIM), jnp.bfloat16)

    scatter_keys(0)
    scatter_values(0)
    scatter_keys(1)
    scatter_values(1)
    forward(0, 0)
    scatter_queries(0)
    forward(1, 0)
    scatter_keys(2)
    relay(0, 0)
    relay(1, 0)
    forward(0, 1)
    scatter_values(2)
    relay(0, 1)
    forward(1, 1)
    scatter_queries(1)
    relay(1, 1)
    gather_context(0)
    attend(0)
    forward(0, 2)
    relay(0, 2)
    forward(1, 2)
    scatter_queries(2)
    relay(1, 2)
    gather_context(1)
    attend(1)
    lat_copy.wait()
    steps_copy.wait()
    update_whole(0)
    gather_context(2)
    attend(2)
    update_whole(1)

    update_ahead()

    def fin_copy(i):
        return pltpu.make_async_remote_copy(
            src_ref=fin_stage.at[i],
            dst_ref=fin_land,
            send_sem=send_f,
            recv_sem=recv_f,
            device_id=(i, h),
            device_id_type=MESH,
        )

    @pl.when(q == N_QUEUE - 1)
    def _():
        fin_stage[:, TOKENS:, :] = jnp.zeros((N_QUEUE, PAD - TOKENS, HEAD_DIM), jnp.bfloat16)
        for i in range(SHARES):
            block = slice(i * HEAD_DIM, (i + 1) * HEAD_DIM)
            wide = jnp.concatenate(
                [leave[j, 0:TOKENS, block].astype(jnp.float32) for j in range(CLASSES)], axis=1
            )
            for p in range(4):
                piece = wide[:, p * COLUMNS:(p + 1) * COLUMNS].astype(jnp.bfloat16)
                fin_stage[4 * i + p, 0:TOKENS, 0:COLUMNS] = piece
                fin_stage[4 * i + p, 0:TOKENS, COLUMNS:] = jnp.zeros(
                    (TOKENS, HEAD_DIM - COLUMNS), jnp.bfloat16
                )

        @pl.loop(0, N_QUEUE - 1)
        def _(i):
            fin_copy(i).start()

        fin_ref[...] = fin_stage[N_QUEUE - 1, 0:TOKENS, 0:COLUMNS]

    update_rest()

    @pl.when(q == 0)
    def _():
        noise_copy.wait()

    @pl.when(q > 0)
    def _():
        for j in range(CLASSES):
            frame_copy(j).wait_recv()
            for i in range(SHARES):
                head = slice((i * CLASSES + j) * HEAD_DIM, (i * CLASSES + j + 1) * HEAD_DIM)
                next_ref[0, :, head] = arrive[j, 0:TOKENS, i * HEAD_DIM:(i + 1) * HEAD_DIM]

    @pl.when(q < N_QUEUE - 1)
    def _():
        await_recv(fin_land, recv_f)
        fin_ref[...] = fin_land[0:TOKENS, 0:COLUMNS]

    await_recv(q_hbm, send_q)
    await_recv(k_hbm, send_k)
    await_recv(v_hbm, send_v)
    for j in range(CLASSES):
        await_recv(obuf.at[j], send_o.at[j])

        @pl.when(has_right)
        def _():
            await_recv(own(kbuf, j), send_n.at[0, 0, j])
            await_recv(own(vbuf, j), send_n.at[1, 0, j])

        @pl.when(has_left)
        def _():
            await_recv(own(kbuf, j), send_n.at[0, 1, j])
            await_recv(own(vbuf, j), send_n.at[1, 1, j])

        @pl.when(is_relay)
        def _():
            await_recv(relayed.at[0, j], send_r.at[0, j])
            await_recv(relayed.at[1, j], send_r.at[1, j])

        @pl.when(q < N_QUEUE - 1)
        def _():
            frame_copy(j).wait_send()

    @pl.when(q == N_QUEUE - 1)
    def _():
        await_recv(fin_stage.at[pl.ds(0, N_QUEUE - 1)], send_f)


def place(next_in, den_in, fin_in, next_out, den_out, fin_out, sems):
    copies = [
        pltpu.make_async_copy(source, target, sems.at[n])
        for n, (source, target) in enumerate(((next_in, next_out), (den_in, den_out), (fin_in, fin_out)))
    ]
    for copy in copies:
        copy.start()
    for copy in copies:
        copy.wait()


def shards(latents, queries, key_proj, values, slot_steps, noise_frame):
    def flat(array):
        return array.reshape(ROWS, D)

    hbm = pl.BlockSpec(memory_space=pltpu.HBM)
    vmem = pl.BlockSpec(memory_space=pltpu.VMEM)
    bf16 = jnp.bfloat16
    dma = pltpu.SemaphoreType.DMA
    results = pl.pallas_call(
        kernel,
        out_shape=(
            jax.ShapeDtypeStruct((FRAMES, TOKENS, D), bf16),
            jax.ShapeDtypeStruct((FRAMES, TOKENS, D), bf16),
            jax.ShapeDtypeStruct((TOKENS, COLUMNS), bf16),
        ),
        in_specs=[hbm] * 6,
        out_specs=(vmem, vmem, vmem),
        scratch_shapes=[
            pltpu.VMEM((CLASSES, WINDOW, HEAD_DIM), bf16),
            pltpu.VMEM((CLASSES, CONTEXT, HEAD_DIM), bf16),
            pltpu.VMEM((CLASSES, CONTEXT, HEAD_DIM), bf16),
            pltpu.VMEM((CLASSES, WINDOW, HEAD_DIM), bf16),
            pltpu.VMEM((CLASSES, ROWS, SHARES * HEAD_DIM), bf16),
            pltpu.VMEM((ROWS, D), bf16),
            pltpu.VMEM((CLASSES, PAD, SHARES * HEAD_DIM), bf16),
            pltpu.VMEM((CLASSES, PAD, SHARES * HEAD_DIM), bf16),
            pltpu.VMEM((N_QUEUE, PAD, HEAD_DIM), bf16),
            pltpu.VMEM((PAD, HEAD_DIM), bf16),
            pltpu.VMEM((2, CLASSES, PIECE, HEAD_DIM), bf16),
            pltpu.SMEM((FRAMES,), jnp.int32),
            dma, dma, dma,
            dma((CLASSES, WINDOW // CHUNK)), dma((CLASSES,)), dma((CLASSES,)),
            dma((2, 2, CLASSES)), dma((2, 2, CLASSES)), dma((2, CLASSES)), dma((2, CLASSES)),
            dma((CLASSES,)), dma((CLASSES + 1,)),
            dma((CLASSES,)), dma((CLASSES,)),
            dma, dma, dma, dma, dma,
        ],
        compiler_params=pltpu.CompilerParams(
            collective_id=0, has_side_effects=True, vmem_limit_bytes=48 * 1024 * 1024
        ),
    )(*(pltpu.with_memory_space_constraint(a, pltpu.HBM) for a in (flat(queries), flat(key_proj), flat(values), flat(latents), noise_frame, slot_steps)))


    anywhere = pl.BlockSpec(memory_space=pl.ANY)
    return pl.pallas_call(
        place,
        out_shape=tuple(jax.ShapeDtypeStruct(r.shape, r.dtype) for r in results),
        in_specs=[vmem] * 3,
        out_specs=(anywhere,) * 3,
        scratch_shapes=[dma((3,))],
    )(*(pltpu.with_memory_space_constraint(r, pltpu.VMEM) for r in results))


def solution(mesh):
    spec = P("queue", "head", None)
    return jax.shard_map(
        shards,
        mesh=mesh,
        in_specs=(spec, spec, spec, spec, P("queue"), P("head", None)),
        out_specs=(spec, spec, P("head", "queue")),
        check_vma=False,
    )
```

```python
import functools
import math

import jax
import jax.numpy as jnp
from jax import lax
from jax.experimental import pallas as pl
from jax.experimental.pallas import tpu as pltpu
from jax.sharding import PartitionSpec as P

MESH = pl.DeviceIdType.MESH
HEADS = 24
HEAD_DIM = 128
D = HEADS * HEAD_DIM
FRAMES = 4
TOKENS = 24
ROWS = FRAMES * TOKENS
SHARES = 8
CLASSES = 3
WINDOW = ROWS * SHARES
CONTEXT = 3 * WINDOW
N_QUEUE = 32
STEPS = 128
HALF = N_QUEUE // 2
CHUNK = 192
PIECE = WINDOW // 4
PAD = 32
REST = ROWS - PAD
LAST = CLASSES - 1
AHEAD = SHARES * PAD
COLUMNS = D // N_QUEUE
SCALE = math.log2(math.e) / math.sqrt(HEAD_DIM)
shift_factor = 3.0


def noise_level(step_index):
    fraction = 1.0 - step_index / float(STEPS)
    return shift_factor * fraction / (1.0 + (shift_factor - 1.0) * fraction)


def kernel(
    q_hbm, k_hbm, v_hbm, lat_hbm, noise_hbm, steps_hbm,
    next_ref, den_ref, fin_ref,
    qbuf, kbuf, vbuf, obuf, vel, lat, leave, arrive, fin_stage, fin_land, relayed, steps_ref,
    send_q, send_k, send_v, recv_q, recv_k, recv_v,
    send_n, recv_n, send_r, recv_r,
    send_o, recv_o, send_l, recv_l, send_f, recv_f, lat_sem, noise_sem, steps_sem,
):
    q = lax.axis_index("queue")
    h = lax.axis_index("head")
    y, z_hi = h // 2, h % 2
    z_lo = q // 8
    far = (q + HALF) % N_QUEUE

    def flip(window):
        return (window // 16) % 2

    s_mine = (z_hi + flip(far)) % 2
    site_id = y * 2 + s_mine
    window = far

    def site_of(win, ident):
        return ((win + HALF) % N_QUEUE, (ident // 2) * 2 + (ident + flip(win)) % 2)

    group, place = window // 8, window % 8
    has_left = window > 0
    has_right = window < N_QUEUE - 1
    last = jnp.logical_and(place == 7, has_right)
    first = jnp.logical_and(place == 0, has_left)
    plain_right = place < 7
    plain_left = place > 0
    up = jnp.logical_and(jnp.logical_and(place % 2 == 1, place < 7), group < 3)
    down = jnp.logical_and(jnp.logical_and(place % 2 == 0, place > 0), group > 0)
    is_relay = jnp.logical_or(up, down)
    relay_from = site_of(jnp.where(up, 8 * group + 7, 8 * group), site_id)
    relay_to = site_of(jnp.where(up, 8 * group + 8, (8 * group + N_QUEUE - 1) % N_QUEUE) % N_QUEUE, site_id)

    def relay_up(grp, p):
        return site_of((8 * grp + 2 * p + 1) % N_QUEUE, site_id)

    def relay_down(grp, p):
        return site_of((8 * grp + 2 * p) % N_QUEUE, site_id)

    left_site = site_of((window + N_QUEUE - 1) % N_QUEUE, site_id)
    right_site = site_of((window + 1) % N_QUEUE, site_id)

    lat_copy = pltpu.make_async_copy(lat_hbm, lat, lat_sem)
    lat_copy.start()
    steps_copy = pltpu.make_async_copy(steps_hbm, steps_ref, steps_sem)
    steps_copy.start()
    noise_copy = pltpu.make_async_copy(noise_hbm, next_ref.at[0], noise_sem)

    @pl.when(q == 0)
    def _():
        noise_copy.start()

    barrier = pltpu.get_barrier_semaphore()

    def greet(device):
        pl.semaphore_signal(barrier, inc=1, device_id=device, device_id_type=MESH)

    @pl.loop(0, SHARES)
    def _(i):
        greet((far, i))

    @pl.when(has_left)
    def _():
        greet(left_site)

    @pl.when(has_right)
    def _():
        greet(right_site)

    @pl.when(last)
    def _():
        for p in range(3):
            greet(relay_down(group + 1, p + 1))

    @pl.when(first)
    def _():
        for p in range(3):
            greet(relay_up(group + 3, p))

    @pl.when(is_relay)
    def _():
        greet(relay_from)

    @pl.when(q > 0)
    def _():
        greet((q - 1, h))

    @pl.when(q < N_QUEUE - 1)
    def _():
        greet((N_QUEUE - 1, h))

    edges = SHARES + has_left.astype(jnp.int32) + has_right.astype(jnp.int32)
    edges = edges + 3 * last.astype(jnp.int32) + 3 * first.astype(jnp.int32) + is_relay.astype(jnp.int32)
    edges = edges + (q < N_QUEUE - 1).astype(jnp.int32)
    edges = edges + (N_QUEUE - 1) * (q == N_QUEUE - 1).astype(jnp.int32)
    pl.semaphore_wait(barrier, edges)

    def scatter(src, dst, send, recv, j, row0):
        @pl.loop(0, SHARES)
        def _(n):
            i = (2 * y + n) % SHARES
            column = pl.multiple_of((i * CLASSES + j) * HEAD_DIM, HEAD_DIM)
            row = pl.multiple_of(row0 + h * ROWS, 16)
            pltpu.make_async_remote_copy(
                src_ref=src.at[:, pl.ds(column, HEAD_DIM)],
                dst_ref=dst.at[j, pl.ds(row, ROWS), :],
                send_sem=send,
                recv_sem=recv,
                device_id=site_of(q, i),
                device_id_type=MESH,
            ).start()

    def scatter_keys(j):
        scatter(k_hbm, kbuf, send_k, recv_k.at[j], j, WINDOW)

    def scatter_values(j):
        scatter(v_hbm, vbuf, send_v, recv_v.at[j], j, WINDOW)

    def scatter_queries(j):
        if j < LAST:
            scatter(q_hbm, qbuf, send_q, recv_q.at[j, y], j, 0)
            return
        for rows, start, place_of, sem in (
            (PAD, REST, h * PAD, recv_q.at[j, 0]),
            (REST, 0, AHEAD + h * REST, recv_q.at[j, 1 + h // 4]),
        ):
            @pl.loop(0, SHARES)
            def _(n):
                i = (2 * y + n) % SHARES
                column = pl.multiple_of((i * CLASSES + j) * HEAD_DIM, HEAD_DIM)
                pltpu.make_async_remote_copy(
                    src_ref=q_hbm.at[pl.ds(start, rows), pl.ds(column, HEAD_DIM)],
                    dst_ref=qbuf.at[j, pl.ds(pl.multiple_of(place_of, 16), rows), :],
                    send_sem=send_q,
                    recv_sem=sem,
                    device_id=site_of(q, i),
                    device_id_type=MESH,
                ).start()

    def await_recv(ref, sem):
        pltpu.make_async_copy(ref, ref, sem).wait()

    def own(buf, j):
        return buf.at[j, pl.ds(WINDOW, WINDOW), :]

    def pass_on(n, buf, j, side, device, base, start, rows):
        return pltpu.make_async_remote_copy(
            src_ref=buf.at[j, pl.ds(WINDOW + start, rows), :],
            dst_ref=buf.at[j, pl.ds(base + start, rows), :],
            send_sem=send_n.at[n, side, j],
            recv_sem=recv_n.at[n, side, j],
            device_id=device,
            device_id_type=MESH,
        )

    def by_relay(n, buf, j, side, device, start):
        return pltpu.make_async_remote_copy(
            src_ref=buf.at[j, pl.ds(WINDOW + start, PIECE), :],
            dst_ref=relayed.at[n, j],
            send_sem=send_n.at[n, side, j],
            recv_sem=recv_r.at[n, j],
            device_id=device,
            device_id_type=MESH,
        )

    def forward(n, j):
        buf, recv = ((kbuf, recv_k), (vbuf, recv_v))[n]
        await_recv(own(buf, j), recv.at[j])

        @pl.when(plain_right)
        def _():
            pass_on(n, buf, j, 0, right_site, 0, 0, WINDOW).start()

        @pl.when(plain_left)
        def _():
            pass_on(n, buf, j, 1, left_site, 2 * WINDOW, 0, WINDOW).start()

        @pl.when(last)
        def _():
            pass_on(n, buf, j, 0, right_site, 0, 3 * PIECE, PIECE).start()
            for p in range(3):
                by_relay(n, buf, j, 0, relay_up(group, p), p * PIECE).start()

        @pl.when(first)
        def _():
            pass_on(n, buf, j, 1, left_site, 2 * WINDOW, 0, PIECE).start()
            for p in range(3):
                by_relay(n, buf, j, 1, relay_down(group, p + 1), (p + 1) * PIECE).start()

    def relay(n, j):
        buf = (kbuf, vbuf)[n]

        @pl.when(is_relay)
        def _():
            side = jnp.where(up, 0, 1)
            row = pl.multiple_of(jnp.where(up, 0, 2 * WINDOW) + place // 2 * PIECE, 16)
            await_recv(relayed.at[n, j], recv_r.at[n, j])
            pltpu.make_async_remote_copy(
                src_ref=relayed.at[n, j],
                dst_ref=buf.at[j, pl.ds(row, PIECE), :],
                send_sem=send_r.at[n, j],
                recv_sem=recv_n.at[n, side, j],
                device_id=relay_to,
                device_id_type=MESH,
            ).start()

    left_flag = has_left.astype(jnp.float32)
    right_flag = has_right.astype(jnp.float32)

    def gather_context(j):
        @pl.when(has_left)
        def _():
            await_recv(kbuf.at[j, pl.ds(0, WINDOW), :], recv_n.at[0, 0, j])
            await_recv(vbuf.at[j, pl.ds(0, WINDOW), :], recv_n.at[1, 0, j])

        @pl.when(jnp.logical_not(has_left))
        def _():
            kbuf[j, 0:WINDOW, :] = kbuf[j, WINDOW:2 * WINDOW, :]
            vbuf[j, 0:WINDOW, :] = jnp.zeros((WINDOW, HEAD_DIM), jnp.bfloat16)

        @pl.when(has_right)
        def _():
            await_recv(kbuf.at[j, pl.ds(2 * WINDOW, WINDOW), :], recv_n.at[0, 1, j])
            await_recv(vbuf.at[j, pl.ds(2 * WINDOW, WINDOW), :], recv_n.at[1, 1, j])

        @pl.when(jnp.logical_not(has_right))
        def _():
            kbuf[j, 2 * WINDOW:, :] = kbuf[j, WINDOW:2 * WINDOW, :]
            vbuf[j, 2 * WINDOW:, :] = jnp.zeros((WINDOW, HEAD_DIM), jnp.bfloat16)

    def attend_rows(j, rows):
        scores = lax.dot_general(
            qbuf[j, rows, :], kbuf[j], (((1,), (1,)), ((), ())),
            preferred_element_type=jnp.float32,
        )
        top = jnp.max(scores, axis=1, keepdims=True)
        weights = jnp.exp2((scores - top) * SCALE)
        total = (
            left_flag * jnp.sum(weights[:, :WINDOW], axis=1, keepdims=True)
            + jnp.sum(weights[:, WINDOW:2 * WINDOW], axis=1, keepdims=True)
            + right_flag * jnp.sum(weights[:, 2 * WINDOW:], axis=1, keepdims=True)
        )
        mixed = jnp.dot(
            weights.astype(jnp.bfloat16), vbuf[j], preferred_element_type=jnp.float32
        )
        obuf[j, rows, :] = (mixed / total).astype(jnp.bfloat16)

    def attend(j):
        if j < LAST:
            @pl.loop(0, WINDOW // CHUNK)
            def _(n):
                c = (y + n) % (WINDOW // CHUNK)
                rows = pl.ds(pl.multiple_of(c * CHUNK, CHUNK), CHUNK)
                await_recv(qbuf.at[j, rows, :], recv_q.at[j, c])
                attend_rows(j, rows)
                for i in range(CHUNK // ROWS):
                    share = c * (CHUNK // ROWS) + i
                    give_back(j, share, pl.multiple_of(share * ROWS, 16), 0, ROWS, 0)
            return

        ahead = pl.ds(0, AHEAD)
        await_recv(qbuf.at[j, ahead, :], recv_q.at[j, 0])
        attend_rows(j, ahead)

        @pl.loop(0, SHARES)
        def _(n):
            share = (2 * y + n) % SHARES
            give_back(j, share, pl.multiple_of(share * PAD, 16), REST, PAD, 0)

        @pl.loop(0, 2)
        def _(n):
            c = (y // 2 + n) % 2
            rows = pl.ds(pl.multiple_of(AHEAD + c * 4 * REST, 16), 4 * REST)
            await_recv(qbuf.at[j, rows, :], recv_q.at[j, 1 + c])
            attend_rows(j, rows)
            for i in range(4):
                share = 4 * c + i
                give_back(j, share, pl.multiple_of(AHEAD + share * REST, 16), 0, REST, 1)

    def give_back(j, share, row, start, rows, part):
        column = pl.multiple_of(site_id * HEAD_DIM, HEAD_DIM)
        pltpu.make_async_remote_copy(
            src_ref=obuf.at[j, pl.ds(row, rows), :],
            dst_ref=vel.at[j, pl.ds(start, rows), pl.ds(column, HEAD_DIM)],
            send_sem=send_o.at[j],
            recv_sem=recv_o.at[j + part],
            device_id=(far, share),
            device_id_type=MESH,
        ).start()

    def levels():
        now, change = [], []
        for f in range(FRAMES):
            step = jnp.full((TOKENS, HEAD_DIM), steps_ref[f], jnp.int32)
            level = noise_level(step.astype(jnp.float32))
            level_next = noise_level((step + 1).astype(jnp.float32))
            now.append(level)
            change.append(level_next - level)
        return now, change

    def update(j, frames):
        now, change = levels()
        for i in range(SHARES):
            head = slice((i * CLASSES + j) * HEAD_DIM, (i * CLASSES + j + 1) * HEAD_DIM)
            block = slice(i * HEAD_DIM, (i + 1) * HEAD_DIM)
            base = REST if min(frames) == FRAMES - 1 else 0
            speed = vel[j, base:, block].astype(jnp.float32)
            latent = lat[base:, head].astype(jnp.float32)
            for f in frames:
                frame = slice(f * TOKENS - base, (f + 1) * TOKENS - base)
                updated = (latent[frame] + change[f] * speed[frame]).astype(jnp.bfloat16)
                den_ref[f, :, head] = (latent[frame] - now[f] * speed[frame]).astype(jnp.bfloat16)
                if f < FRAMES - 1:
                    next_ref[f + 1, :, head] = updated
                else:
                    leave[j, 0:TOKENS, block] = updated

        if FRAMES - 1 in frames:
            @pl.when(q < N_QUEUE - 1)
            def _():
                frame_copy(j).start()

    def update_whole(j):
        await_recv(obuf.at[j], recv_o.at[j])
        update(j, range(FRAMES))

    def update_ahead():
        await_recv(obuf.at[LAST, pl.ds(0, AHEAD), :], recv_o.at[LAST])
        update(LAST, (FRAMES - 1,))

    def update_rest():
        await_recv(obuf.at[LAST, pl.ds(AHEAD, WINDOW - AHEAD), :], recv_o.at[LAST + 1])
        update(LAST, range(FRAMES - 1))

    def frame_copy(j):
        return pltpu.make_async_remote_copy(
            src_ref=leave.at[j],
            dst_ref=arrive.at[j],
            send_sem=send_l.at[j],
            recv_sem=recv_l.at[j],
            device_id=((q + 1) % N_QUEUE, h),
            device_id_type=MESH,
        )

    leave[:, TOKENS:, :] = jnp.zeros((CLASSES, PAD - TOKENS, SHARES * HEAD_DIM), jnp.bfloat16)

    scatter_keys(0)
    scatter_values(0)
    scatter_keys(1)
    scatter_values(1)
    forward(0, 0)
    scatter_queries(0)
    forward(1, 0)
    scatter_keys(2)
    relay(0, 0)
    relay(1, 0)
    forward(0, 1)
    scatter_values(2)
    relay(0, 1)
    forward(1, 1)
    scatter_queries(1)
    relay(1, 1)
    gather_context(0)
    attend(0)
    forward(0, 2)
    relay(0, 2)
    forward(1, 2)
    scatter_queries(2)
    relay(1, 2)
    gather_context(1)
    attend(1)
    lat_copy.wait()
    steps_copy.wait()
    update_whole(0)
    gather_context(2)
    attend(2)
    update_whole(1)

    update_ahead()

    def fin_copy(i):
        return pltpu.make_async_remote_copy(
            src_ref=fin_stage.at[i],
            dst_ref=fin_land,
            send_sem=send_f,
            recv_sem=recv_f,
            device_id=(i, h),
            device_id_type=MESH,
        )

    @pl.when(q == N_QUEUE - 1)
    def _():
        fin_stage[:, TOKENS:, :] = jnp.zeros((N_QUEUE, PAD - TOKENS, HEAD_DIM), jnp.bfloat16)
        for i in range(SHARES):
            block = slice(i * HEAD_DIM, (i + 1) * HEAD_DIM)
            wide = jnp.concatenate(
                [leave[j, 0:TOKENS, block].astype(jnp.float32) for j in range(CLASSES)], axis=1
            )
            for p in range(4):
                piece = wide[:, p * COLUMNS:(p + 1) * COLUMNS].astype(jnp.bfloat16)
                fin_stage[4 * i + p, 0:TOKENS, 0:COLUMNS] = piece
                fin_stage[4 * i + p, 0:TOKENS, COLUMNS:] = jnp.zeros(
                    (TOKENS, HEAD_DIM - COLUMNS), jnp.bfloat16
                )

        @pl.loop(0, N_QUEUE - 1)
        def _(i):
            fin_copy(i).start()

        fin_ref[...] = fin_stage[N_QUEUE - 1, 0:TOKENS, 0:COLUMNS]

    def take_frame(classes):
        @pl.when(q > 0)
        def _():
            for j in classes:
                frame_copy(j).wait_recv()
                for i in range(SHARES):
                    head = slice((i * CLASSES + j) * HEAD_DIM, (i * CLASSES + j + 1) * HEAD_DIM)
                    next_ref[0, :, head] = arrive[j, 0:TOKENS, i * HEAD_DIM:(i + 1) * HEAD_DIM]

    take_frame(range(LAST))
    update_rest()

    @pl.when(q == 0)
    def _():
        noise_copy.wait()

    take_frame((LAST,))

    @pl.when(q < N_QUEUE - 1)
    def _():
        await_recv(fin_land, recv_f)
        fin_ref[...] = fin_land[0:TOKENS, 0:COLUMNS]

    await_recv(q_hbm, send_q)
    await_recv(k_hbm, send_k)
    await_recv(v_hbm, send_v)
    for j in range(CLASSES):
        await_recv(obuf.at[j], send_o.at[j])

        @pl.when(has_right)
        def _():
            await_recv(own(kbuf, j), send_n.at[0, 0, j])
            await_recv(own(vbuf, j), send_n.at[1, 0, j])

        @pl.when(has_left)
        def _():
            await_recv(own(kbuf, j), send_n.at[0, 1, j])
            await_recv(own(vbuf, j), send_n.at[1, 1, j])

        @pl.when(is_relay)
        def _():
            await_recv(relayed.at[0, j], send_r.at[0, j])
            await_recv(relayed.at[1, j], send_r.at[1, j])

        @pl.when(q < N_QUEUE - 1)
        def _():
            frame_copy(j).wait_send()

    @pl.when(q == N_QUEUE - 1)
    def _():
        await_recv(fin_stage.at[pl.ds(0, N_QUEUE - 1)], send_f)


def place(next_in, den_in, fin_in, next_out, den_out, fin_out, sems):
    copies = [
        pltpu.make_async_copy(source, target, sems.at[n])
        for n, (source, target) in enumerate(((next_in, next_out), (den_in, den_out), (fin_in, fin_out)))
    ]
    for copy in copies:
        copy.start()
    for copy in copies:
        copy.wait()


def shards(latents, queries, key_proj, values, slot_steps, noise_frame):
    def flat(array):
        return array.reshape(ROWS, D)

    hbm = pl.BlockSpec(memory_space=pltpu.HBM)
    vmem = pl.BlockSpec(memory_space=pltpu.VMEM)
    bf16 = jnp.bfloat16
    dma = pltpu.SemaphoreType.DMA
    results = pl.pallas_call(
        kernel,
        out_shape=(
            jax.ShapeDtypeStruct((FRAMES, TOKENS, D), bf16),
            jax.ShapeDtypeStruct((FRAMES, TOKENS, D), bf16),
            jax.ShapeDtypeStruct((TOKENS, COLUMNS), bf16),
        ),
        in_specs=[hbm] * 6,
        out_specs=(vmem, vmem, vmem),
        scratch_shapes=[
            pltpu.VMEM((CLASSES, WINDOW, HEAD_DIM), bf16),
            pltpu.VMEM((CLASSES, CONTEXT, HEAD_DIM), bf16),
            pltpu.VMEM((CLASSES, CONTEXT, HEAD_DIM), bf16),
            pltpu.VMEM((CLASSES, WINDOW, HEAD_DIM), bf16),
            pltpu.VMEM((CLASSES, ROWS, SHARES * HEAD_DIM), bf16),
            pltpu.VMEM((ROWS, D), bf16),
            pltpu.VMEM((CLASSES, PAD, SHARES * HEAD_DIM), bf16),
            pltpu.VMEM((CLASSES, PAD, SHARES * HEAD_DIM), bf16),
            pltpu.VMEM((N_QUEUE, PAD, HEAD_DIM), bf16),
            pltpu.VMEM((PAD, HEAD_DIM), bf16),
            pltpu.VMEM((2, CLASSES, PIECE, HEAD_DIM), bf16),
            pltpu.SMEM((FRAMES,), jnp.int32),
            dma, dma, dma,
            dma((CLASSES, WINDOW // CHUNK)), dma((CLASSES,)), dma((CLASSES,)),
            dma((2, 2, CLASSES)), dma((2, 2, CLASSES)), dma((2, CLASSES)), dma((2, CLASSES)),
            dma((CLASSES,)), dma((CLASSES + 1,)),
            dma((CLASSES,)), dma((CLASSES,)),
            dma, dma, dma, dma, dma,
        ],
        compiler_params=pltpu.CompilerParams(
            collective_id=0, has_side_effects=True, vmem_limit_bytes=48 * 1024 * 1024
        ),
    )(*(pltpu.with_memory_space_constraint(a, pltpu.HBM) for a in (flat(queries), flat(key_proj), flat(values), flat(latents), noise_frame, slot_steps)))


    anywhere = pl.BlockSpec(memory_space=pl.ANY)
    return pl.pallas_call(
        place,
        out_shape=tuple(jax.ShapeDtypeStruct(r.shape, r.dtype) for r in results),
        in_specs=[vmem] * 3,
        out_specs=(anywhere,) * 3,
        scratch_shapes=[dma((3,))],
    )(*(pltpu.with_memory_space_constraint(r, pltpu.VMEM) for r in results))


def solution(mesh):
    spec = P("queue", "head", None)
    return jax.shard_map(
        shards,
        mesh=mesh,
        in_specs=(spec, spec, spec, spec, P("queue"), P("head", None)),
        out_specs=(spec, spec, P("head", "queue")),
        check_vma=False,
    )
```
